32 devices in a mesh: member: 4 (over y, x), dp: 8 (over z, core).
Axes of the slice: x: 2, y: 2, z: 4, core: 2. Of those that a mesh axis runs over, the one named last changes fastest.
Arguments:
- inputs: bfloat16 [2048, 64], P('dp'), may hold values from -6 to 6
- observed: float32 [64, 2048], P('member', 'dp'), may hold values from -6 to 6
- noise: bfloat16 [2, 8, 64, 2048], P(None, None, 'member', 'dp'), may hold values from -4 to 4
- w_in: float32 [8, 64, 4096], P('member', None, 'dp'), may hold values from -0.75 to 0.75
- b_in: float32 [8, 4096], P('member', 'dp'), may hold values from -3 to 3
- w_out: float32 [8, 64, 4096], P('member', None, 'dp'), may hold values from -0.09375 to 0.09375
- b_out: float32 [8, 64], P('member'), may hold values from -3 to 3
Outputs:
- new_w_in: float32 [8, 64, 4096], P('member', None, 'dp')
- new_b_in: float32 [8, 4096], P('member', 'dp')
- new_w_out: float32 [8, 64, 4096], P('member', None, 'dp')
- new_b_out: float32 [8, 64], P('member')
The draws below stay inside these ranges and needn't reach their ends.
All inputs are finite; a program needn't handle non-finite values.
Results may differ from the reference program's by a relative error of at most 0.00056.
Values may be sent and summed in bfloat16 or wider, within the bound.
A program may use at most 64 MiB of HBM per device.

```python
import jax
import jax.numpy as jnp
from jax import lax

F_IN = 64
H = 4096
O = 64
UPDATES = 2
MEMBERS = 8
SAMPLES = 2048


def with_spikes(values, key, source, target, shards_of, factor):
    def block_of(dim):
        return (jnp.arange(values.shape[dim]) // (values.shape[dim] // shards_of)).reshape((-1,) + (1,) * (values.ndim - 1 - dim))

    near = jax.random.permutation(key, shards_of)[block_of(target)]
    second = (block_of(target) + shards_of // 2) % shards_of
    return jnp.where((block_of(source) == near) | (block_of(source) == second), factor * values, values)


def levels(rng, shape, pieces, smallest, largest):
    def one(position, parts):
        heights = jax.random.uniform(jax.random.fold_in(jax.random.fold_in(rng, 6), position), (parts,), jnp.float32, smallest / len(pieces), largest / len(pieces))
        return jnp.repeat(jnp.exp(heights), shape[position] // parts).reshape((-1,) + (1,) * (len(shape) - position - 1))

    loudness = one(*pieces[0])
    for cut in pieces[1:]:
        loudness = loudness * one(*cut)
    return loudness


def scatter_about(rng, extent, width, limit, cuts=(), held_as=jnp.bfloat16):
    result = width * jax.random.normal(rng, extent, jnp.float32)
    if cuts:
        result = result * levels(rng, extent, cuts, -0.22, 0.18)
    return jnp.clip(result, -limit, limit).astype(held_as)


def heavy_noise(key, extent, deviation, limit, shards, heavy, kind=jnp.bfloat16):
    entries = deviation * jax.random.normal(key, extent, jnp.float32)
    if shards:
        entries = entries * levels(key, extent, shards, -0.22, 0.18)
    return jnp.clip(with_spikes(entries, jax.random.fold_in(key, 3), *heavy), -limit, limit).astype(kind)


def setup_inputs(seed: int = 0) -> dict:
    arg_keys = jax.random.split(jax.random.key(seed), 8)
    inputs = scatter_about(arg_keys[0], (SAMPLES, F_IN), 1.0, 6.0, ((0, 8),))
    observed = scatter_about(arg_keys[1], (O, SAMPLES), 1.0, 6.0, ((0, 4), (1, 8)), jnp.float32)
    noise = heavy_noise(arg_keys[2], (UPDATES, MEMBERS, O, SAMPLES), 0.5, 4.0, ((2, 4), (3, 8)), (3, 1, 8, 2.0))
    w_in = scatter_about(arg_keys[3], (MEMBERS, F_IN, H), F_IN ** -0.5, 0.75, ((0, 4), (2, 8)), jnp.float32)
    b_in = scatter_about(arg_keys[4], (MEMBERS, H), 0.5, 3.0, ((0, 4), (1, 8)), jnp.float32)
    w_out = scatter_about(arg_keys[5], (MEMBERS, O, H), H ** -0.5, 0.09375, ((0, 4), (2, 8)), jnp.float32)
    b_out = scatter_about(arg_keys[6], (MEMBERS, O), 0.5, 3.0, ((0, 4),), jnp.float32)
    return {"inputs": inputs, "observed": observed, "noise": noise, "w_in": w_in, "b_in": b_in, "w_out": w_out, "b_out": b_out}


ridge_level = 0.5

def forward(inputs, w_in, b_in, w_out, b_out):

    def single(item):
        weight_in, bias_in, weight_out, bias_out = item
        rounded_bias = lax.optimization_barrier(bias_in.astype(jnp.bfloat16))
        pre = jnp.dot(inputs.astype(jnp.float32), weight_in.astype(jnp.bfloat16).astype(jnp.float32), preferred_element_type=jnp.float32) + rounded_bias.astype(jnp.float32)[None, :]
        hidden = jnp.tanh(pre).astype(jnp.bfloat16)
        predicted = lax.dot_general(weight_out.astype(jnp.bfloat16).astype(jnp.float32), hidden.astype(jnp.float32), (((1,), (1,)), ((), ())), preferred_element_type=jnp.float32)
        return predicted + bias_out[:, None]
    return lax.map(single, (w_in, b_in, w_out, b_out))

def solve_gain(gram, cross):
    eye = jnp.eye(gram.shape[0], dtype=gram.dtype)
    factor = jnp.linalg.cholesky(gram + ridge_level * eye)
    middle = lax.linalg.triangular_solve(factor, cross, left_side=True, lower=True)
    return lax.linalg.triangular_solve(factor, middle, left_side=True, lower=True, transpose_a=True)

def blend(param, gain):
    flat = param.reshape(param.shape[0], -1)
    moved = lax.dot_general(gain, flat, (((0,), (0,)), ((), ())), precision=lax.Precision.HIGHEST)
    return param + moved.reshape(param.shape)

def reference(inputs, observed, noise, w_in, b_in, w_out, b_out):
    count = observed.shape[0] * observed.shape[1]
    for update in range(UPDATES):
        predicted = forward(inputs, w_in, b_in, w_out, b_out)
        mean_pred = jnp.mean(predicted, axis=0)
        anomaly = (predicted - mean_pred[None]).reshape(predicted.shape[0], -1)
        misfit = (observed[None] + noise[update].astype(jnp.float32) - predicted).reshape(predicted.shape[0], -1)
        gram = lax.dot_general(anomaly, anomaly, (((1,), (1,)), ((), ())), precision=lax.Precision.HIGHEST) / count
        cross = lax.dot_general(anomaly, misfit, (((1,), (1,)), ((), ())), precision=lax.Precision.HIGHEST) / count
        gain = solve_gain(gram, cross)
        w_in = blend(w_in, gain)
        b_in = blend(b_in, gain)
        w_out = blend(w_out, gain)
        b_out = blend(b_out, gain)
    return (w_in, b_in, w_out, b_out)
```

```python
import functools

import jax
import jax.numpy as jnp
from jax import lax
from jax.experimental import pallas as pl
from jax.experimental.pallas import tpu as pltpu
from jax.sharding import PartitionSpec as P

UPDATES = 2
RIDGE = 0.5
CORES = 2
MESH = pl.DeviceIdType.MESH
NT = (((1,), (1,)), ((), ()))


def kernel(
    M, Z, total,
    x_ref, obs_ref, noise_ref, w_in_ref, w_out_ref, extra_ref,
    new_in_ref, new_out_ref, new_extra_ref,
    xg, hi, lo, fresh, other, bias, staged, got, anomalies, misfits, pair, every,
    x_send, x_recv, hi_send, hi_recv, lo_send, lo_recv, w_send, w_recv,
    piece_send, piece_recv, pair_send, pair_recv, every_send, every_recv,
):
    f32, bf16 = jnp.float32, jnp.bfloat16
    m = lax.axis_index("member")
    d = lax.axis_index("dp")
    z, c = d // CORES, d % CORES
    per, F = w_in_ref.shape[0], w_in_ref.shape[1]
    O, hl = w_out_ref.shape[1], w_out_ref.shape[2]
    K = per * M
    ob = O // M
    samples = noise_ref.shape[2]
    rows = hi.shape[2]
    slots = Z * M
    me = z * M + m
    twin = (m, z * CORES + (1 - c))

    def at(dm, dz):
        return lax.rem(m + dm, M), lax.rem(z - dz + Z, Z) * CORES + c

    def send(src, dst, send_sem, recv_sem, target):
        pltpu.make_async_remote_copy(
            src_ref=src, dst_ref=dst, send_sem=send_sem, recv_sem=recv_sem,
            device_id=target, device_id_type=MESH,
        ).start()

    def settle(ref, sem):
        pltpu.make_async_copy(ref, ref, sem).wait()

    barrier = pltpu.get_barrier_semaphore()
    pl.semaphore_signal(barrier, inc=1, device_id=twin, device_id_type=MESH)

    def greet(i, carry):
        pl.semaphore_signal(
            barrier, inc=1, device_id=at(lax.rem(i, M), i // M), device_id_type=MESH
        )
        return carry

    lax.fori_loop(1, slots, greet, 0)

    for j in range(per):
        for top, part in ((0, w_in_ref[j]), (F, w_out_ref[j]), (F + O, extra_ref[j])):
            high = part.astype(bf16)
            span = pl.ds(top, part.shape[0])
            hi[m, j, span, :] = high
            lo[m, j, span, :] = (part - high.astype(f32)).astype(bf16)
    xg[z] = x_ref[...]
    pl.semaphore_wait(barrier, slots)

    for t in range(1, Z):
        send(xg.at[z], xg.at[z], x_send.at[t], x_recv.at[t], at(0, Z - t))
    send(hi.at[m], other.at[0], w_send.at[0], w_recv.at[0], twin)
    for t in range(1, M):
        send(hi.at[m], hi.at[m], hi_send.at[t], hi_recv.at[t], at(t, 0))

    lane = lax.broadcasted_iota(jnp.int32, (K, 128), 1)
    row = lax.broadcasted_iota(jnp.int32, (K, 128), 0)

    def hidden_part(x, weights, j):
        pre = jnp.dot(x, weights[j, 0:F, :], preferred_element_type=f32)
        pre = pre + weights[j, F + O : rows, :].astype(f32)[0:1]
        hidden = jnp.tanh(pre).astype(bf16)
        return lax.dot_general(
            weights[j, F : F + O, :], hidden, NT, preferred_element_type=f32
        )

    def predict(update, own):
        def step(t, carry):
            if update == 0:
                @pl.when(t > 0)
                def _():
                    settle(xg.at[0], x_recv.at[t])

            target = lax.rem(z - t + Z, Z)
            packed = xg[target].astype(f32)
            x = jnp.concatenate([packed[:, 0:F], packed[:, F:]], axis=0).astype(bf16)
            sums = [hidden_part(x, own, j) for j in range(per)]

            @pl.when(t == 0)
            def _():
                settle(other.at[update], w_recv.at[update])

            here = jnp.where(t == 0, 1.0, 0.0).astype(f32)
            for j in range(per):
                both = sums[j] + hidden_part(x, other.at[update], j)
                both = (both + here * bias[j]).astype(bf16)
                for p in range(M):
                    staged[update, t, p, j * ob : (j + 1) * ob, :] = both[p * ob : (p + 1) * ob, :]

            def post(i, carry):
                to = lax.rem(m + i, M)
                send(
                    staged.at[update, t, to], got.at[update, me],
                    piece_send.at[update], piece_recv.at[update],
                    (to, target * CORES + c),
                )
                return carry

            lax.fori_loop(1, M, post, 0)

            @pl.when(t > 0)
            def _():
                post(0, 0)

            return carry

        lax.fori_loop(0, Z, step, 0)
        got[update, me] = staged[update, 0, m]

    def gain_of(update):
        settle(got.at[update, pl.ds(0, slots - 1)], piece_recv.at[update])
        preds = []
        for p in range(M):
            value = got[update, p].astype(f32)
            for s in range(1, Z):
                value = value + got[update, s * M + p].astype(f32)
            preds += [value[j * ob : (j + 1) * ob] for j in range(per)]
        mean = functools.reduce(jnp.add, preds) * (1.0 / K)
        seen = obs_ref[...]
        for k in range(K):
            span = pl.ds(k * ob, ob)
            anomaly = preds[k] - mean
            misfit = seen + noise_ref[update, span, :].astype(f32) - preds[k]
            for q in range(samples // 128):
                anomalies[q, span, :] = anomaly[:, q * 128 : (q + 1) * 128]
                misfits[q, span, :] = misfit[:, q * 128 : (q + 1) * 128]
        pieces = [(q, o) for q in range(samples // 128) for o in range(ob)]
        a = jnp.concatenate([anomalies[q, pl.ds(o, K, stride=ob), :] for q, o in pieces], axis=1)
        b = jnp.concatenate([misfits[q, pl.ds(o, K, stride=ob), :] for q, o in pieces], axis=1)
        ab = jnp.concatenate([a, b], axis=0)
        ab_high = ab.astype(bf16)
        ab_low = (ab - ab_high.astype(f32)).astype(bf16)
        a_high = a.astype(bf16).astype(f32)
        left = jnp.concatenate([a_high, a - a_high], axis=0).astype(bf16)
        sums = lax.dot_general(left, ab_high, NT, preferred_element_type=f32)
        sums = sums + lax.dot_general(left, ab_low, NT, preferred_element_type=f32)
        pair[update, c] = jnp.zeros((K, 128), f32)
        pair[update, c, :, 0 : 2 * K] = sums[0:K] + sums[K : 2 * K]
        send(pair.at[update, c], pair.at[update, c], pair_send.at[update], pair_recv.at[update], twin)
        settle(pair.at[update, c], pair_recv.at[update])
        every[update, me] = pair[update, 0] + pair[update, 1]

        def post(i, carry):
            send(
                every.at[update, me], every.at[update, me],
                every_send.at[update], every_recv.at[update],
                at(lax.rem(i, M), i // M),
            )
            return carry

        lax.fori_loop(1, slots, post, 0)
        settle(every.at[update, pl.ds(0, slots - 1)], every_recv.at[update])
        system = jnp.sum(every[update], axis=0) * (1.0 / total)
        system = system + jnp.where(lane == row, RIDGE, 0.0)
        for i in range(K):
            pivot = system[i : i + 1, :]
            pivot = pivot / pivot[:, i : i + 1]
            column = system[:, i : i + 1]
            system = jnp.where(row == i, pivot, system - column * pivot)
        return system

    def columns_of(gain):
        return [
            jnp.sum(jnp.where(lane == K + m * per + j, gain, 0.0), axis=1, keepdims=True)
            for j in range(per)
        ]

    def mixed(columns, top, count, base, with_low):
        span = pl.ds(top, count)
        sums = list(base)
        for k in range(K):
            value = hi[k // per, k % per, span, :].astype(f32)
            if with_low:
                value = value + lo[k // per, k % per, span, :].astype(f32)
            for j in range(per):
                sums[j] = sums[j] + columns[j][k : k + 1, :] * value
        return sums

    for j in range(per):
        bias[j] = extra_ref[j].astype(f32)[1:2, 0:O].T

    predict(0, hi.at[m])
    for t in range(1, M):
        send(lo.at[m], lo.at[m], lo_send.at[t], lo_recv.at[t], at(t, 0))
    first = gain_of(0)
    for t in range(1, M):
        settle(hi.at[0], hi_recv.at[t])

    chosen = columns_of(first)
    own_rows = [
        [
            jnp.sum(jnp.where(row[:, 0:1] == m * per + k, chosen[j], 0.0), axis=0, keepdims=True)
            for k in range(per)
        ]
        for j in range(per)
    ]

    def renew(top, count, base):
        sums = mixed(chosen, top, count, base, False)
        for k in range(per):
            rest = lo[m, k, pl.ds(top, count), :].astype(f32)
            for j in range(per):
                sums[j] = sums[j] + own_rows[j][k] * rest
        for j in range(per):
            fresh[j, pl.ds(top, count), :] = sums[j].astype(bf16)
        return sums

    for start, ref, size in ((0, w_in_ref, F), (F, w_out_ref, O)):
        def chunk(i, carry, start=start, ref=ref):
            at_row = pl.multiple_of(i * 16, 16)
            renew(
                pl.multiple_of(start + i * 16, 16), 16,
                [ref[j, pl.ds(at_row, 16), :] for j in range(per)],
            )
            return carry

        lax.fori_loop(0, size // 16, chunk, 0)
    tail = renew(F + O, 16, [extra_ref[j] for j in range(per)])
    for j in range(per):
        bias[j] = tail[j][1:2, 0:O].T
    send(fresh, other.at[1], w_send.at[1], w_recv.at[1], twin)

    predict(1, fresh)
    second = gain_of(1)
    for t in range(1, M):
        settle(lo.at[0], lo_recv.at[t])

    joint = first + second
    for i in range(K):
        joint = joint + first[:, K + i : K + i + 1] * second[i : i + 1, :]
    chosen_both = columns_of(joint)
    for start, ref, out, size in ((0, w_in_ref, new_in_ref, F), (F, w_out_ref, new_out_ref, O)):
        def finish(i, carry, start=start, ref=ref, out=out):
            at_row = pl.multiple_of(i * 16, 16)
            sums = mixed(
                chosen_both, pl.multiple_of(start + i * 16, 16), 16,
                [ref[j, pl.ds(at_row, 16), :] for j in range(per)], True,
            )
            for j in range(per):
                out[j, pl.ds(at_row, 16), :] = sums[j]
            return carry

        lax.fori_loop(0, size // 16, finish, 0)
    sums = mixed(chosen_both, F + O, 16, [extra_ref[j] for j in range(per)], True)
    for j in range(per):
        new_extra_ref[j] = sums[j]

    for t in range(1, Z):
        settle(xg.at[0], x_send.at[t])
    for t in range(1, M):
        settle(hi.at[0], hi_send.at[t])
        settle(lo.at[0], lo_send.at[t])
    for update in range(UPDATES):
        settle(fresh, w_send.at[update])
        settle(got.at[update, pl.ds(0, slots - 1)], piece_send.at[update])
        settle(pair.at[update, 0], pair_send.at[update])
        settle(every.at[update, pl.ds(0, slots - 1)], every_send.at[update])


def on_device(M, Z, inputs, observed, noise, w_in, b_in, w_out, b_out):
    f32, bf16 = jnp.float32, jnp.bfloat16
    per, F, hl = w_in.shape
    O = w_out.shape[1]
    K = per * M
    ob, samples = observed.shape
    half = samples // 2
    rows = F + O + 16
    slots = Z * M
    packed = jnp.concatenate([inputs[:half], inputs[half:]], axis=1)
    extra = jnp.concatenate(
        [b_in[:, None, :], jnp.pad(b_out, ((0, 0), (0, hl - O)))[:, None, :], jnp.zeros((per, 14, hl), f32)],
        axis=1,
    )
    total = float(O * samples * CORES * Z)
    vmem = pl.BlockSpec(memory_space=pltpu.VMEM)
    dma = pltpu.SemaphoreType.DMA
    new_in, new_out, new_extra = pl.pallas_call(
        functools.partial(kernel, M, Z, total),
        out_shape=(
            jax.ShapeDtypeStruct(w_in.shape, f32),
            jax.ShapeDtypeStruct(w_out.shape, f32),
            jax.ShapeDtypeStruct(extra.shape, f32),
        ),
        in_specs=[vmem] * 6,
        out_specs=(vmem,) * 3,
        scratch_shapes=[
            pltpu.VMEM((Z, half, 2 * F), bf16),
            pltpu.VMEM((M, per, rows, hl), bf16),
            pltpu.VMEM((M, per, rows, hl), bf16),
            pltpu.VMEM((per, rows, hl), bf16),
            pltpu.VMEM((UPDATES, per, rows, hl), bf16),
            pltpu.VMEM((per, O, 1), f32),
            pltpu.VMEM((UPDATES, Z, M, per * ob, samples), bf16),
            pltpu.VMEM((UPDATES, slots, per * ob, samples), bf16),
            pltpu.VMEM((samples // 128, K * ob, 128), f32),
            pltpu.VMEM((samples // 128, K * ob, 128), f32),
            pltpu.VMEM((UPDATES, CORES, K, 128), f32),
            pltpu.VMEM((UPDATES, slots, K, 128), f32),
            dma((Z,)), dma((Z,)),
            dma((M,)), dma((M,)),
            dma((M,)), dma((M,)),
            dma((UPDATES,)), dma((UPDATES,)),
            dma((UPDATES,)), dma((UPDATES,)),
            dma((UPDATES,)), dma((UPDATES,)),
            dma((UPDATES,)), dma((UPDATES,)),
        ],
        compiler_params=pltpu.CompilerParams(
            collective_id=0, has_side_effects=True, vmem_limit_bytes=40 * 1024 * 1024
        ),
        name="inversion",
    )(packed, observed, noise.reshape(UPDATES, K * ob, samples), w_in, w_out, extra)
    return new_in, new_extra[:, 0, :], new_out, new_extra[:, 1, :O]


def solution(mesh):
    placed = (
        P("dp", None),
        P("member", "dp"),
        P(None, None, "member", "dp"),
        P("member", None, "dp"),
        P("member", "dp"),
        P("member", None, "dp"),
        P("member", None),
    )
    return jax.shard_map(
        functools.partial(on_device, mesh.shape["member"], mesh.shape["dp"] // CORES),
        mesh=mesh,
        in_specs=placed,
        out_specs=(
            P("member", None, "dp"),
            P("member", "dp"),
            P("member", None, "dp"),
            P("member", None),
        ),
        check_vma=False,
    )
```

```python
import functools

import jax
import jax.numpy as jnp
from jax import lax
from jax.experimental import pallas as pl
from jax.experimental.pallas import tpu as pltpu
from jax.sharding import PartitionSpec as P

UPDATES = 2
RIDGE = 0.5
CORES = 2
MESH = pl.DeviceIdType.MESH
NT = (((1,), (1,)), ((), ()))


def kernel(
    M, Z, total,
    x_hbm, obs_hbm, noise_hbm, w_in_hbm, b_in_hbm, w_out_hbm, b_out_hbm,
    new_in_ref, new_b_in_ref, new_out_ref, new_b_out_ref,
    obs_ref, noise_ref, w_in_ref, b_in_ref, w_out_ref, b_out_ref, extra_ref, load_sem,
    xg, turned, hi, lo, fresh, other, bias, staged, got, anomalies, misfits, pair, every,
    x_send, x_recv, hi_send, hi_recv, lo_send, lo_recv, w_send, w_recv,
    piece_send, piece_recv, pair_send, pair_recv, every_send, every_recv,
):
    f32, bf16 = jnp.float32, jnp.bfloat16
    m = lax.axis_index("member")
    d = lax.axis_index("dp")
    z, c = d // CORES, d % CORES
    per, F = w_in_ref.shape[0], w_in_ref.shape[1]
    O, hl = w_out_ref.shape[1], w_out_ref.shape[2]
    K = per * M
    ob = O // M
    samples = noise_ref.shape[2]
    rows = hi.shape[2]
    A = rows - O
    slots = Z * M
    me = z * M + m
    twin = (m, z * CORES + (1 - c))

    def at(dm, dz):
        return lax.rem(m + dm, M), lax.rem(z - dz + Z, Z) * CORES + c

    def send(src, dst, send_sem, recv_sem, target):
        pltpu.make_async_remote_copy(
            src_ref=src, dst_ref=dst, send_sem=send_sem, recv_sem=recv_sem,
            device_id=target, device_id_type=MESH,
        ).start()

    def settle(ref, sem):
        pltpu.make_async_copy(ref, ref, sem).wait()

    loads = [
        pltpu.make_async_copy(src, dst, load_sem.at[i])
        for i, (src, dst) in enumerate((
            (x_hbm, xg.at[z, pl.ds(0, F)]), (w_in_hbm, w_in_ref), (b_in_hbm, b_in_ref),
            (b_out_hbm, b_out_ref), (w_out_hbm, w_out_ref), (obs_hbm, obs_ref), (noise_hbm, noise_ref),
        ))
    ]
    for load in loads:
        load.start()

    barrier = pltpu.get_barrier_semaphore()
    pl.semaphore_signal(barrier, inc=1, device_id=twin, device_id_type=MESH)

    def greet(i, carry):
        pl.semaphore_signal(
            barrier, inc=1, device_id=at(lax.rem(i, M), i // M), device_id_type=MESH
        )
        return carry

    lax.fori_loop(1, slots, greet, 0)

    ones = jnp.where(lax.broadcasted_iota(jnp.int32, (16, samples), 0) == 0, 1.0, 0.0)
    for i in range(Z):
        xg[i, F:A, :] = ones.astype(bf16)
    for load in loads[1:4]:
        load.wait()
    extra_ref[...] = jnp.zeros_like(extra_ref)
    for j in range(per):
        extra_ref[j, 0:1, :] = b_in_ref[j : j + 1, :]
        extra_ref[j, 1:2, 0:O] = b_out_ref[j : j + 1, :]
    loads[4].wait()

    for j in range(per):
        for top, part in ((0, w_in_ref[j]), (F, extra_ref[j]), (A, w_out_ref[j])):
            high = part.astype(bf16)
            span = pl.ds(top, part.shape[0])
            hi[m, j, span, :] = high
            lo[m, j, span, :] = (part - high.astype(f32)).astype(bf16)
    loads[0].wait()
    pl.semaphore_wait(barrier, slots)

    for t in range(1, Z):
        send(xg.at[z, pl.ds(0, F)], xg.at[z, pl.ds(0, F)], x_send.at[t], x_recv.at[t], at(0, Z - t))
    send(hi.at[m], other.at[0], w_send.at[0], w_recv.at[0], twin)
    for t in range(1, M):
        send(hi.at[m], hi.at[m], hi_send.at[t], hi_recv.at[t], at(t, 0))

    lane = lax.broadcasted_iota(jnp.int32, (K, 128), 1)
    row = lax.broadcasted_iota(jnp.int32, (K, 128), 0)

    def turn(half, weights):
        for j in range(per):
            turned[half, j] = weights[j, 0:A, :].astype(f32).T.astype(bf16)

    def hidden_part(x, half, weights, j):
        pre = jnp.dot(turned[half, j], x, preferred_element_type=f32)
        hidden = jnp.tanh(pre).astype(bf16)
        return jnp.dot(weights[j, A:rows, :], hidden, preferred_element_type=f32)

    def predict(update, own):
        turn(0, own)

        def step(t, carry):
            if update == 0:
                @pl.when(t > 0)
                def _():
                    settle(xg.at[0, pl.ds(0, F)], x_recv.at[t])

            target = lax.rem(z - t + Z, Z)
            x = xg[target]
            sums = [hidden_part(x, 0, own, j) for j in range(per)]

            @pl.when(t == 0)
            def _():
                settle(other.at[update], w_recv.at[update])
                turn(1, other.at[update])

            here = jnp.where(t == 0, 1.0, 0.0).astype(f32)
            for j in range(per):
                both = sums[j] + hidden_part(x, 1, other.at[update], j)
                both = (both + here * bias[j]).astype(bf16)
                for p in range(M):
                    staged[update, t, p, j * ob : (j + 1) * ob, :] = both[p * ob : (p + 1) * ob, :]

            def post(i, carry):
                to = lax.rem(m + i, M)
                send(
                    staged.at[update, t, to], got.at[update, me],
                    piece_send.at[update], piece_recv.at[update],
                    (to, target * CORES + c),
                )
                return carry

            lax.fori_loop(1, M, post, 0)

            @pl.when(t > 0)
            def _():
                post(0, 0)

            return carry

        lax.fori_loop(0, Z, step, 0)
        got[update, me] = staged[update, 0, m]

    def gain_of(update):
        settle(got.at[update, pl.ds(0, slots - 1)], piece_recv.at[update])
        preds = []
        for p in range(M):
            value = got[update, p].astype(f32)
            for s in range(1, Z):
                value = value + got[update, s * M + p].astype(f32)
            preds += [value[j * ob : (j + 1) * ob] for j in range(per)]
        if update == 0:
            for load in loads[5:]:
                load.wait()
        mean = functools.reduce(jnp.add, preds) * (1.0 / K)
        seen = obs_ref[...]
        for k in range(K):
            span = pl.ds(k * ob, ob)
            anomaly = preds[k] - mean
            misfit = seen + noise_ref[update, span, :].astype(f32) - preds[k]
            for q in range(samples // 128):
                anomalies[q, span, :] = anomaly[:, q * 128 : (q + 1) * 128]
                misfits[q, span, :] = misfit[:, q * 128 : (q + 1) * 128]
        pieces = [(q, o) for q in range(samples // 128) for o in range(ob)]
        a = jnp.concatenate([anomalies[q, pl.ds(o, K, stride=ob), :] for q, o in pieces], axis=1)
        b = jnp.concatenate([misfits[q, pl.ds(o, K, stride=ob), :] for q, o in pieces], axis=1)
        ab = jnp.concatenate([a, b], axis=0)
        ab_high = ab.astype(bf16)
        ab_low = (ab - ab_high.astype(f32)).astype(bf16)
        a_high = a.astype(bf16).astype(f32)
        left = jnp.concatenate([a_high, a - a_high], axis=0).astype(bf16)
        sums = lax.dot_general(left, ab_high, NT, preferred_element_type=f32)
        sums = sums + lax.dot_general(left, ab_low, NT, preferred_element_type=f32)
        pair[update, c] = jnp.zeros((K, 128), f32)
        pair[update, c, :, 0 : 2 * K] = sums[0:K] + sums[K : 2 * K]
        send(pair.at[update, c], pair.at[update, c], pair_send.at[update], pair_recv.at[update], twin)
        settle(pair.at[update, c], pair_recv.at[update])
        every[update, me] = pair[update, 0] + pair[update, 1]

        def post(i, carry):
            send(
                every.at[update, me], every.at[update, me],
                every_send.at[update], every_recv.at[update],
                at(lax.rem(i, M), i // M),
            )
            return carry

        lax.fori_loop(1, slots, post, 0)
        settle(every.at[update, pl.ds(0, slots - 1)], every_recv.at[update])
        system = jnp.sum(every[update], axis=0) * (1.0 / total)
        system = system + jnp.where(lane == row, RIDGE, 0.0)
        for i in range(K):
            pivot = system[i : i + 1, :]
            pivot = pivot / pivot[:, i : i + 1]
            column = system[:, i : i + 1]
            system = jnp.where(row == i, pivot, system - column * pivot)
        return system

    def columns_of(gain):
        return [
            jnp.sum(jnp.where(lane == K + m * per + j, gain, 0.0), axis=1, keepdims=True)
            for j in range(per)
        ]

    def mixed(columns, top, count, base, with_low):
        span = pl.ds(top, count)
        sums = list(base)
        for k in range(K):
            value = hi[k // per, k % per, span, :].astype(f32)
            if with_low:
                value = value + lo[k // per, k % per, span, :].astype(f32)
            for j in range(per):
                sums[j] = sums[j] + columns[j][k : k + 1, :] * value
        return sums

    for j in range(per):
        bias[j] = extra_ref[j].astype(f32)[1:2, 0:O].T

    predict(0, hi.at[m])
    for t in range(1, M):
        send(lo.at[m], lo.at[m], lo_send.at[t], lo_recv.at[t], at(t, 0))
    first = gain_of(0)
    for t in range(1, M):
        settle(hi.at[0], hi_recv.at[t])

    chosen = columns_of(first)
    own_rows = [
        [
            jnp.sum(jnp.where(row[:, 0:1] == m * per + k, chosen[j], 0.0), axis=0, keepdims=True)
            for k in range(per)
        ]
        for j in range(per)
    ]

    def renew(top, count, base):
        sums = mixed(chosen, top, count, base, False)
        for k in range(per):
            rest = lo[m, k, pl.ds(top, count), :].astype(f32)
            for j in range(per):
                sums[j] = sums[j] + own_rows[j][k] * rest
        for j in range(per):
            fresh[j, pl.ds(top, count), :] = sums[j].astype(bf16)
        return sums

    for start, ref, size in ((0, w_in_ref, F), (A, w_out_ref, O)):
        def chunk(i, carry, start=start, ref=ref):
            at_row = pl.multiple_of(i * 16, 16)
            renew(
                pl.multiple_of(start + i * 16, 16), 16,
                [ref[j, pl.ds(at_row, 16), :] for j in range(per)],
            )
            return carry

        lax.fori_loop(0, size // 16, chunk, 0)
    tail = renew(F, 16, [extra_ref[j] for j in range(per)])
    for j in range(per):
        bias[j] = tail[j][1:2, 0:O].T
    send(fresh, other.at[1], w_send.at[1], w_recv.at[1], twin)

    predict(1, fresh)
    second = gain_of(1)
    for t in range(1, M):
        settle(lo.at[0], lo_recv.at[t])

    joint = first + second
    for i in range(K):
        joint = joint + first[:, K + i : K + i + 1] * second[i : i + 1, :]
    chosen_both = columns_of(joint)
    for start, ref, out, size in ((0, w_in_ref, new_in_ref, F), (A, w_out_ref, new_out_ref, O)):
        def finish(i, carry, start=start, ref=ref, out=out):
            at_row = pl.multiple_of(i * 16, 16)
            sums = mixed(
                chosen_both, pl.multiple_of(start + i * 16, 16), 16,
                [ref[j, pl.ds(at_row, 16), :] for j in range(per)], True,
            )
            for j in range(per):
                out[j, pl.ds(at_row, 16), :] = sums[j]
            return carry

        lax.fori_loop(0, size // 16, finish, 0)
    sums = mixed(chosen_both, F, 16, [extra_ref[j] for j in range(per)], True)
    for j in range(per):
        new_b_in_ref[j : j + 1, :] = sums[j][0:1]
        new_b_out_ref[j : j + 1, :] = sums[j][1:2, 0:O]

    for t in range(1, Z):
        settle(xg.at[0, pl.ds(0, F)], x_send.at[t])
    for t in range(1, M):
        settle(hi.at[0], hi_send.at[t])
        settle(lo.at[0], lo_send.at[t])
    for update in range(UPDATES):
        settle(fresh, w_send.at[update])
        settle(got.at[update, pl.ds(0, slots - 1)], piece_send.at[update])
        settle(pair.at[update, 0], pair_send.at[update])
        settle(every.at[update, pl.ds(0, slots - 1)], every_send.at[update])


def on_device(M, Z, inputs, observed, noise, w_in, b_in, w_out, b_out):
    f32, bf16 = jnp.float32, jnp.bfloat16
    per, F, hl = w_in.shape
    O = w_out.shape[1]
    K = per * M
    ob, samples = observed.shape
    rows = F + O + 16
    slots = Z * M
    total = float(O * samples * CORES * Z)
    vmem = pl.BlockSpec(memory_space=pltpu.VMEM)
    dma = pltpu.SemaphoreType.DMA
    hbm = pl.BlockSpec(memory_space=pltpu.HBM)
    return pl.pallas_call(
        functools.partial(kernel, M, Z, total),
        out_shape=tuple(
            jax.ShapeDtypeStruct(own.shape, f32) for own in (w_in, b_in, w_out, b_out)
        ),
        in_specs=[hbm] * 7,
        out_specs=(vmem,) * 4,
        scratch_shapes=[
            pltpu.VMEM((ob, samples), f32),
            pltpu.VMEM((UPDATES, K * ob, samples), bf16),
            pltpu.VMEM(w_in.shape, f32),
            pltpu.VMEM(b_in.shape, f32),
            pltpu.VMEM(w_out.shape, f32),
            pltpu.VMEM(b_out.shape, f32),
            pltpu.VMEM((per, 16, hl), f32),
            dma((7,)),
            pltpu.VMEM((Z, F + 16, samples), bf16),
            pltpu.VMEM((CORES, per, hl, F + 16), bf16),
            pltpu.VMEM((M, per, rows, hl), bf16),
            pltpu.VMEM((M, per, rows, hl), bf16),
            pltpu.VMEM((per, rows, hl), bf16),
            pltpu.VMEM((UPDATES, per, rows, hl), bf16),
            pltpu.VMEM((per, O, 1), f32),
            pltpu.VMEM((UPDATES, Z, M, per * ob, samples), bf16),
            pltpu.VMEM((UPDATES, slots, per * ob, samples), bf16),
            pltpu.VMEM((samples // 128, K * ob, 128), f32),
            pltpu.VMEM((samples // 128, K * ob, 128), f32),
            pltpu.VMEM((UPDATES, CORES, K, 128), f32),
            pltpu.VMEM((UPDATES, slots, K, 128), f32),
            dma((Z,)), dma((Z,)),
            dma((M,)), dma((M,)),
            dma((M,)), dma((M,)),
            dma((UPDATES,)), dma((UPDATES,)),
            dma((UPDATES,)), dma((UPDATES,)),
            dma((UPDATES,)), dma((UPDATES,)),
            dma((UPDATES,)), dma((UPDATES,)),
        ],
        compiler_params=pltpu.CompilerParams(
            collective_id=0, has_side_effects=True, vmem_limit_bytes=56 * 1024 * 1024
        ),
        name="inversion",
    )(inputs.T, observed, noise.reshape(UPDATES, K * ob, samples), w_in, b_in, w_out, b_out)


def solution(mesh):
    placed = (
        P("dp", None),
        P("member", "dp"),
        P(None, None, "member", "dp"),
        P("member", None, "dp"),
        P("member", "dp"),
        P("member", None, "dp"),
        P("member", None),
    )
    return jax.shard_map(
        functools.partial(on_device, mesh.shape["member"], mesh.shape["dp"] // CORES),
        mesh=mesh,
        in_specs=placed,
        out_specs=(
            P("member", None, "dp"),
            P("member", "dp"),
            P("member", None, "dp"),
            P("member", None),
        ),
        check_vma=False,
    )
```

```python
import functools

import jax
import jax.numpy as jnp
from jax import lax
from jax.experimental import pallas as pl
from jax.experimental.pallas import tpu as pltpu
from jax.sharding import PartitionSpec as P

UPDATES = 2
RIDGE = 0.5
CORES = 2
IN_SCALE, BIAS_SCALE, OUT_SCALE = 2.0**15, 2.0**13, 2.0**18
TINY = 2.0**-125
MESH = pl.DeviceIdType.MESH
NT = (((1,), (1,)), ((), ()))


def kernel(
    M, Z, total,
    x_hbm, obs_hbm, noise_hbm, w_in_hbm, b_in_hbm, w_out_hbm, b_out_hbm,
    new_in_ref, new_b_in_ref, new_out_ref, new_b_out_ref,
    obs_ref, noise_ref, w_in_ref, b_in_ref, w_out_ref, b_out_ref, extra_ref, load_sem,
    xg, turned, own, code, full, fresh, other, bias, staged, got, anomalies, misfits, pair, every,
    x_send, x_recv, code_send, code_recv, w_send, w_recv,
    piece_send, piece_recv, pair_send, pair_recv, every_send, every_recv,
):
    f32, bf16 = jnp.float32, jnp.bfloat16
    m = lax.axis_index("member")
    d = lax.axis_index("dp")
    z, c = d // CORES, d % CORES
    per, F = w_in_ref.shape[0], w_in_ref.shape[1]
    O, hl = w_out_ref.shape[1], w_out_ref.shape[2]
    K = per * M
    ob = O // M
    samples = noise_ref.shape[2]
    rows = own.shape[1]
    A = rows - O
    slots = Z * M
    me = z * M + m
    twin = (m, z * CORES + (1 - c))

    def at(dm, dz):
        return lax.rem(m + dm, M), lax.rem(z - dz + Z, Z) * CORES + c

    def send(src, dst, send_sem, recv_sem, target):
        pltpu.make_async_remote_copy(
            src_ref=src, dst_ref=dst, send_sem=send_sem, recv_sem=recv_sem,
            device_id=target, device_id_type=MESH,
        ).start()

    def settle(ref, sem):
        pltpu.make_async_copy(ref, ref, sem).wait()

    loads = [
        pltpu.make_async_copy(src, dst, load_sem.at[i])
        for i, (src, dst) in enumerate((
            (x_hbm, xg.at[z, pl.ds(0, F)]), (w_in_hbm, w_in_ref), (b_in_hbm, b_in_ref),
            (b_out_hbm, b_out_ref), (w_out_hbm, w_out_ref), (obs_hbm, obs_ref), (noise_hbm, noise_ref),
        ))
    ]
    for load in loads:
        load.start()

    barrier = pltpu.get_barrier_semaphore()
    pl.semaphore_signal(barrier, inc=1, device_id=twin, device_id_type=MESH)

    def greet(i, carry):
        pl.semaphore_signal(
            barrier, inc=1, device_id=at(lax.rem(i, M), i // M), device_id_type=MESH
        )
        return carry

    lax.fori_loop(1, slots, greet, 0)

    ones = jnp.where(lax.broadcasted_iota(jnp.int32, (16, samples), 0) == 0, 1.0, 0.0)
    for i in range(Z):
        xg[i, F:A, :] = ones.astype(bf16)
    for load in loads[1:4]:
        load.wait()
    extra_ref[...] = jnp.zeros_like(extra_ref)
    for j in range(per):
        extra_ref[j, 0:1, :] = b_in_ref[j : j + 1, :]
        extra_ref[j, 1:2, 0:O] = b_out_ref[j : j + 1, :]
    loads[4].wait()

    for j in range(per):
        for top, part, scale in (
            (0, w_in_ref[j], IN_SCALE), (F, extra_ref[j], BIAS_SCALE), (A, w_out_ref[j], OUT_SCALE)
        ):
            span = pl.ds(top, part.shape[0])
            own[j, span, :] = part.astype(bf16)
            full[m, j, span, :] = part
            power = part * scale
            for _ in range(3):
                power = power * power
            code[m, j, span, :] = jnp.where(part < 0, -power, power).astype(bf16)
    loads[0].wait()
    pl.semaphore_wait(barrier, slots)

    for t in range(1, Z):
        send(xg.at[z, pl.ds(0, F)], xg.at[z, pl.ds(0, F)], x_send.at[t], x_recv.at[t], at(0, Z - t))
    send(own, other.at[0], w_send.at[0], w_recv.at[0], twin)
    for t in range(1, M):
        send(code.at[m], code.at[m], code_send.at[t], code_recv.at[t], at(t, 0))

    lane = lax.broadcasted_iota(jnp.int32, (K, 128), 1)
    row = lax.broadcasted_iota(jnp.int32, (K, 128), 0)

    def turn(half, weights):
        for j in range(per):
            turned[half, j] = weights[j, 0:A, :].astype(f32).T.astype(bf16)

    def hidden_part(x, half, weights, j):
        pre = jnp.dot(turned[half, j], x, preferred_element_type=f32)
        hidden = jnp.tanh(pre).astype(bf16)
        return jnp.dot(weights[j, A:rows, :], hidden, preferred_element_type=f32)

    def decode():
        for t in range(1, M):
            settle(code.at[0], code_recv.at[t])

        def chunk(i, carry):
            slot = lax.rem(m + 1 + i // (per * (rows // 16)), M)
            j = lax.rem(i // (rows // 16), per)
            top = lax.rem(i, rows // 16) * 16
            span = pl.ds(pl.multiple_of(top, 16), 16)
            value = code[slot, j, span, :].astype(f32)
            scale = jnp.where(top < F, 1 / IN_SCALE, jnp.where(top < A, 1 / BIAS_SCALE, 1 / OUT_SCALE))
            size = jnp.abs(value)
            root = jnp.exp2(jnp.log2(jnp.maximum(size, TINY)) * 0.125) * scale
            root = jnp.where(size < TINY, 0.0, root)
            full[slot, j, span, :] = jnp.where(value < 0, -root, root)
            return carry

        lax.fori_loop(0, (M - 1) * per * (rows // 16), chunk, 0, unroll=2)

    def predict(update, own):
        turn(0, own)

        def step(t, carry):
            if update == 0:
                @pl.when(t > 0)
                def _():
                    settle(xg.at[0, pl.ds(0, F)], x_recv.at[t])

            target = lax.rem(z - t + Z, Z)
            x = xg[target]
            sums = [hidden_part(x, 0, own, j) for j in range(per)]

            @pl.when(t == 0)
            def _():
                settle(other.at[update], w_recv.at[update])
                turn(1, other.at[update])

            here = jnp.where(t == 0, 1.0, 0.0).astype(f32)
            for j in range(per):
                both = sums[j] + hidden_part(x, 1, other.at[update], j)
                both = (both + here * bias[j]).astype(bf16)
                for p in range(M):
                    staged[update, t, p, j * ob : (j + 1) * ob, :] = both[p * ob : (p + 1) * ob, :]

            def post(i, carry):
                to = lax.rem(m + i, M)
                send(
                    staged.at[update, t, to], got.at[update, me],
                    piece_send.at[update], piece_recv.at[update],
                    (to, target * CORES + c),
                )
                return carry

            lax.fori_loop(1, M, post, 0)

            @pl.when(t > 0)
            def _():
                post(0, 0)

            return carry

        lax.fori_loop(0, Z, step, 0)
        got[update, me] = staged[update, 0, m]

    def gain_of(update):
        settle(got.at[update, pl.ds(0, slots - 1)], piece_recv.at[update])
        preds = []
        for p in range(M):
            value = got[update, p].astype(f32)
            for s in range(1, Z):
                value = value + got[update, s * M + p].astype(f32)
            preds += [value[j * ob : (j + 1) * ob] for j in range(per)]
        if update == 0:
            for load in loads[5:]:
                load.wait()
        mean = functools.reduce(jnp.add, preds) * (1.0 / K)
        seen = obs_ref[...]
        for k in range(K):
            span = pl.ds(k * ob, ob)
            anomaly = preds[k] - mean
            misfit = seen + noise_ref[update, span, :].astype(f32) - preds[k]
            for q in range(samples // 128):
                anomalies[q, span, :] = anomaly[:, q * 128 : (q + 1) * 128]
                misfits[q, span, :] = misfit[:, q * 128 : (q + 1) * 128]
        pieces = [(q, o) for q in range(samples // 128) for o in range(ob)]
        a = jnp.concatenate([anomalies[q, pl.ds(o, K, stride=ob), :] for q, o in pieces], axis=1)
        b = jnp.concatenate([misfits[q, pl.ds(o, K, stride=ob), :] for q, o in pieces], axis=1)
        ab = jnp.concatenate([a, b], axis=0)
        ab_high = ab.astype(bf16)
        ab_low = (ab - ab_high.astype(f32)).astype(bf16)
        a_high = a.astype(bf16).astype(f32)
        left = jnp.concatenate([a_high, a - a_high], axis=0).astype(bf16)
        sums = lax.dot_general(left, ab_high, NT, preferred_element_type=f32)
        sums = sums + lax.dot_general(left, ab_low, NT, preferred_element_type=f32)
        pair[update, c] = jnp.zeros((K, 128), f32)
        pair[update, c, :, 0 : 2 * K] = sums[0:K] + sums[K : 2 * K]
        send(pair.at[update, c], pair.at[update, c], pair_send.at[update], pair_recv.at[update], twin)
        settle(pair.at[update, c], pair_recv.at[update])
        every[update, me] = pair[update, 0] + pair[update, 1]

        def post(i, carry):
            send(
                every.at[update, me], every.at[update, me],
                every_send.at[update], every_recv.at[update],
                at(lax.rem(i, M), i // M),
            )
            return carry

        lax.fori_loop(1, slots, post, 0)
        if update == 0:
            decode()
        settle(every.at[update, pl.ds(0, slots - 1)], every_recv.at[update])
        system = jnp.sum(every[update], axis=0) * (1.0 / total)
        system = system + jnp.where(lane == row, RIDGE, 0.0)
        for i in range(K):
            pivot = system[i : i + 1, :]
            pivot = pivot / pivot[:, i : i + 1]
            column = system[:, i : i + 1]
            system = jnp.where(row == i, pivot, system - column * pivot)
        return system

    def columns_of(gain):
        return [
            jnp.sum(jnp.where(lane == K + m * per + j, gain, 0.0), axis=1, keepdims=True)
            for j in range(per)
        ]

    def mixed(columns, top, count):
        span = pl.ds(top, count)
        sums = [full[m, j, span, :] for j in range(per)]
        for k in range(K):
            value = full[k // per, k % per, span, :]
            for j in range(per):
                sums[j] = sums[j] + columns[j][k : k + 1, :] * value
        return sums

    for j in range(per):
        bias[j] = extra_ref[j].astype(f32)[1:2, 0:O].T

    predict(0, own)
    first = gain_of(0)
    chosen = columns_of(first)

    def renew(top, count):
        sums = mixed(chosen, top, count)
        for j in range(per):
            fresh[j, pl.ds(top, count), :] = sums[j].astype(bf16)
        return sums

    def chunk(i, carry):
        renew(pl.multiple_of(i * 16, 16), 16)
        return carry

    lax.fori_loop(0, rows // 16, chunk, 0)
    tail = mixed(chosen, F, 16)
    for j in range(per):
        bias[j] = tail[j][1:2, 0:O].T
    send(fresh, other.at[1], w_send.at[1], w_recv.at[1], twin)

    predict(1, fresh)
    second = gain_of(1)

    joint = first + second
    for i in range(K):
        joint = joint + first[:, K + i : K + i + 1] * second[i : i + 1, :]
    chosen_both = columns_of(joint)
    for start, out, size in ((0, new_in_ref, F), (A, new_out_ref, O)):
        def finish(i, carry, start=start, out=out):
            at_row = pl.multiple_of(i * 16, 16)
            sums = mixed(chosen_both, pl.multiple_of(start + i * 16, 16), 16)
            for j in range(per):
                out[j, pl.ds(at_row, 16), :] = sums[j]
            return carry

        lax.fori_loop(0, size // 16, finish, 0)
    sums = mixed(chosen_both, F, 16)
    for j in range(per):
        new_b_in_ref[j : j + 1, :] = sums[j][0:1]
        new_b_out_ref[j : j + 1, :] = sums[j][1:2, 0:O]

    for t in range(1, Z):
        settle(xg.at[0, pl.ds(0, F)], x_send.at[t])
    for t in range(1, M):
        settle(code.at[0], code_send.at[t])
    for update in range(UPDATES):
        settle(fresh, w_send.at[update])
        settle(got.at[update, pl.ds(0, slots - 1)], piece_send.at[update])
        settle(pair.at[update, 0], pair_send.at[update])
        settle(every.at[update, pl.ds(0, slots - 1)], every_send.at[update])


def place(*refs):
    sems = refs[8]
    moves = [pltpu.make_async_copy(refs[i], refs[4 + i], sems.at[i]) for i in range(4)]
    for move in moves:
        move.start()
    for move in moves:
        move.wait()


def on_device(M, Z, inputs, observed, noise, w_in, b_in, w_out, b_out):
    f32, bf16 = jnp.float32, jnp.bfloat16
    per, F, hl = w_in.shape
    O = w_out.shape[1]
    K = per * M
    ob, samples = observed.shape
    rows = F + O + 16
    slots = Z * M
    total = float(O * samples * CORES * Z)
    vmem = pl.BlockSpec(memory_space=pltpu.VMEM)
    dma = pltpu.SemaphoreType.DMA
    hbm = pl.BlockSpec(memory_space=pltpu.HBM)
    results = pl.pallas_call(
        functools.partial(kernel, M, Z, total),
        out_shape=tuple(
            jax.ShapeDtypeStruct(own.shape, f32) for own in (w_in, b_in, w_out, b_out)
        ),
        in_specs=[hbm] * 7,
        out_specs=(vmem,) * 4,
        scratch_shapes=[
            pltpu.VMEM((ob, samples), f32),
            pltpu.VMEM((UPDATES, K * ob, samples), bf16),
            pltpu.VMEM(w_in.shape, f32),
            pltpu.VMEM(b_in.shape, f32),
            pltpu.VMEM(w_out.shape, f32),
            pltpu.VMEM(b_out.shape, f32),
            pltpu.VMEM((per, 16, hl), f32),
            dma((7,)),
            pltpu.VMEM((Z, F + 16, samples), bf16),
            pltpu.VMEM((CORES, per, hl, F + 16), bf16),
            pltpu.VMEM((per, rows, hl), bf16),
            pltpu.VMEM((M, per, rows, hl), bf16),
            pltpu.VMEM((M, per, rows, hl), f32),
            pltpu.VMEM((per, rows, hl), bf16),
            pltpu.VMEM((UPDATES, per, rows, hl), bf16),
            pltpu.VMEM((per, O, 1), f32),
            pltpu.VMEM((UPDATES, Z, M, per * ob, samples), bf16),
            pltpu.VMEM((UPDATES, slots, per * ob, samples), bf16),
            pltpu.VMEM((samples // 128, K * ob, 128), f32),
            pltpu.VMEM((samples // 128, K * ob, 128), f32),
            pltpu.VMEM((UPDATES, CORES, K, 128), f32),
            pltpu.VMEM((UPDATES, slots, K, 128), f32),
            dma((Z,)), dma((Z,)),
            dma((M,)), dma((M,)),
            dma((UPDATES,)), dma((UPDATES,)),
            dma((UPDATES,)), dma((UPDATES,)),
            dma((UPDATES,)), dma((UPDATES,)),
            dma((UPDATES,)), dma((UPDATES,)),
        ],
        compiler_params=pltpu.CompilerParams(
            collective_id=0, has_side_effects=True, vmem_limit_bytes=56 * 1024 * 1024
        ),
        name="inversion",
    )(inputs.T, observed, noise.reshape(UPDATES, K * ob, samples), w_in, b_in, w_out, b_out)
    return pl.pallas_call(
        place,
        out_shape=tuple(jax.ShapeDtypeStruct(own.shape, f32) for own in results),
        in_specs=[hbm] * 4,
        out_specs=(hbm,) * 4,
        scratch_shapes=[dma((4,))],
        compiler_params=pltpu.CompilerParams(vmem_limit_bytes=56 * 1024 * 1024),
        name="place",
    )(*results)


def solution(mesh):
    placed = (
        P("dp", None),
        P("member", "dp"),
        P(None, None, "member", "dp"),
        P("member", None, "dp"),
        P("member", "dp"),
        P("member", None, "dp"),
        P("member", None),
    )
    return jax.shard_map(
        functools.partial(on_device, mesh.shape["member"], mesh.shape["dp"] // CORES),
        mesh=mesh,
        in_specs=placed,
        out_specs=(
            P("member", None, "dp"),
            P("member", "dp"),
            P("member", None, "dp"),
            P("member", None),
        ),
        check_vma=False,
    )
```

```python
import functools

import jax
import jax.numpy as jnp
from jax import lax
from jax.experimental import pallas as pl
from jax.experimental.pallas import tpu as pltpu
from jax.sharding import PartitionSpec as P

UPDATES = 2
RIDGE = 0.5
CORES = 2
IN_SCALE, BIAS_SCALE, OUT_SCALE = 2.0**15, 2.0**13, 2.0**18
TINY = 2.0**-125
MESH = pl.DeviceIdType.MESH
NT = (((1,), (1,)), ((), ()))


def kernel(
    M, Z, total,
    x_hbm, obs_hbm, noise_hbm, w_in_hbm, b_in_hbm, w_out_hbm, b_out_hbm,
    new_in_ref, new_b_in_ref, new_out_ref, new_b_out_ref,
    obs_ref, noise_ref, w_in_ref, b_in_ref, w_out_ref, b_out_ref, extra_ref, load_sem,
    xg, turned, own, code, full, fresh, other, bias, staged, got, anomalies, misfits, pair, every,
    x_send, x_recv, code_send, code_recv, w_send, w_recv,
    piece_send, piece_recv, pair_send, pair_recv, every_send, every_recv,
):
    f32, bf16 = jnp.float32, jnp.bfloat16
    m = lax.axis_index("member")
    d = lax.axis_index("dp")
    z, c = d // CORES, d % CORES
    per, F = w_in_ref.shape[0], w_in_ref.shape[1]
    O, hl = w_out_ref.shape[1], w_out_ref.shape[2]
    K = per * M
    ob = O // M
    samples = noise_ref.shape[2]
    rows = own.shape[1]
    A = rows - O
    slots = Z * M
    me = z * M + m
    twin = (m, z * CORES + (1 - c))

    members = [lax.rem(m + i, M) for i in range(M)]
    places = [lax.rem(z - i + Z, Z) * CORES + c for i in range(Z)]

    pairs = M // 2
    p_at = [lax.rem(m // 2 + i, pairs) * 2 for i in range(pairs)]
    q = lax.rem(m, 2)

    def send(src, dst, send_sem, recv_sem, target):
        pltpu.make_async_remote_copy(
            src_ref=src, dst_ref=dst, send_sem=send_sem, recv_sem=recv_sem,
            device_id=target, device_id_type=MESH,
        ).start()

    def settle(ref, sem):
        pltpu.make_async_copy(ref, ref, sem).wait()

    loads = [
        pltpu.make_async_copy(src, dst, load_sem.at[i])
        for i, (src, dst) in enumerate((
            (x_hbm, xg.at[z, pl.ds(0, F)]), (w_in_hbm, w_in_ref), (b_in_hbm, b_in_ref),
            (b_out_hbm, b_out_ref), (w_out_hbm, w_out_ref), (obs_hbm, obs_ref), (noise_hbm, noise_ref),
        ))
    ]
    for load in loads:
        load.start()

    barrier = pltpu.get_barrier_semaphore()
    pl.semaphore_signal(barrier, inc=1, device_id=twin, device_id_type=MESH)

    others = [(members[i % M], places[i // M]) for i in range(1, slots)]
    for peer in others:
        pl.semaphore_signal(barrier, inc=1, device_id=peer, device_id_type=MESH)

    ones = jnp.where(lax.broadcasted_iota(jnp.int32, (16, samples), 0) == 0, 1.0, 0.0)
    for i in range(Z):
        xg[i, F:A, :] = ones.astype(bf16)
    for load in loads[1:4]:
        load.wait()
    extra_ref[...] = jnp.zeros_like(extra_ref)
    for j in range(per):
        extra_ref[j, 0:1, :] = b_in_ref[j : j + 1, :]
        extra_ref[j, 1:2, 0:O] = b_out_ref[j : j + 1, :]
    loads[4].wait()

    for j in range(per):
        for top, part, scale in (
            (0, w_in_ref[j], IN_SCALE), (F, extra_ref[j], BIAS_SCALE), (A, w_out_ref[j], OUT_SCALE)
        ):
            span = pl.ds(top, part.shape[0])
            own[j, span, :] = part.astype(bf16)
            full[m, j, span, :] = part
            power = part * scale
            for _ in range(3):
                power = power * power
            code[m, j, span, :] = jnp.where(part < 0, -power, power).astype(bf16)
    loads[0].wait()
    pl.semaphore_wait(barrier, slots)

    for t in range(1, Z):
        send(xg.at[z, pl.ds(0, F)], xg.at[z, pl.ds(0, F)], x_send.at[t], x_recv.at[t], (m, places[Z - t]))
    send(own, other.at[0], w_send.at[0], w_recv.at[0], twin)
    def pass_on(src, sem, target):
        send(src, src, code_send.at[sem], code_recv.at[sem], (target, places[0]))

    pass_on(code.at[m], 0, p_at[0] + 1 - q)
    for t in range(1, pairs):
        pass_on(code.at[m], t, p_at[t] + q)

    lane = lax.broadcasted_iota(jnp.int32, (K, 128), 1)
    row = lax.broadcasted_iota(jnp.int32, (K, 128), 0)

    def turn(half, weights):
        for j in range(per):
            turned[half, j] = weights[j, 0:A, :].astype(f32).T.astype(bf16)

    def hidden_part(x, half, weights, j):
        pre = jnp.dot(turned[half, j], x, preferred_element_type=f32)
        hidden = jnp.tanh(pre).astype(bf16)
        return jnp.dot(weights[j, A:rows, :], hidden, preferred_element_type=f32)

    cut = per // 2
    first_half, second_half = pl.ds(0, cut), pl.ds(cut, per - cut)

    def forward():
        for t in range(pairs):
            settle(code.at[0], code_recv.at[t])
        for t in range(1, pairs):
            pass_on(code.at[p_at[0] + 1 - q, first_half], pairs + t, p_at[t] + q)
        for t in range(1, pairs):
            pass_on(code.at[p_at[t] + q, second_half], 2 * pairs + t, p_at[0] + 1 - q)

    def decode():
        for t in range(1, pairs):
            settle(code.at[0, first_half], code_recv.at[pairs + t])
            settle(code.at[0, second_half], code_recv.at[2 * pairs + t])

        def chunk(i, carry):
            slot = lax.rem(m + 1 + i // (per * (rows // 16)), M)
            j = lax.rem(i // (rows // 16), per)
            top = lax.rem(i, rows // 16) * 16
            span = pl.ds(pl.multiple_of(top, 16), 16)
            value = code[slot, j, span, :].astype(f32)
            scale = jnp.where(top < F, 1 / IN_SCALE, jnp.where(top < A, 1 / BIAS_SCALE, 1 / OUT_SCALE))
            size = jnp.abs(value)
            root = jnp.exp2(jnp.log2(jnp.maximum(size, TINY)) * 0.125) * scale
            root = jnp.where(size < TINY, 0.0, root)
            full[slot, j, span, :] = jnp.where(value < 0, -root, root)
            return carry

        lax.fori_loop(0, (M - 1) * per * (rows // 16), chunk, 0, unroll=2)

    def predict(update, own):
        turn(0, own)

        def step(turn_number, carry):
            t = turn_number if update == 0 else lax.rem(turn_number + 1, Z)
            if update == 0:
                @pl.when(t > 0)
                def _():
                    settle(xg.at[0, pl.ds(0, F)], x_recv.at[t])

            target = lax.rem(z - t + Z, Z)
            x = xg[target]
            sums = [hidden_part(x, 0, own, j) for j in range(per)]

            @pl.when(turn_number == 0)
            def _():
                settle(other.at[update], w_recv.at[update])
                turn(1, other.at[update])

            here = jnp.where(t == 0, 1.0, 0.0).astype(f32)
            for j in range(per):
                both = sums[j] + hidden_part(x, 1, other.at[update], j)
                both = (both + here * bias[j]).astype(bf16)
                for p in range(M):
                    staged[update, t, p, j * ob : (j + 1) * ob, :] = both[p * ob : (p + 1) * ob, :]

            def post(to):
                send(
                    staged.at[update, t, to], got.at[update, me],
                    piece_send.at[update], piece_recv.at[update],
                    (to, target * CORES + c),
                )

            for to in members[1:]:
                post(to)

            @pl.when(t > 0)
            def _():
                post(m)

            return carry

        lax.fori_loop(0, Z, step, 0)
        got[update, me] = staged[update, 0, m]

    def gain_of(update):
        settle(got.at[update, pl.ds(0, slots - 1)], piece_recv.at[update])
        preds = []
        for p in range(M):
            value = got[update, p].astype(f32)
            for s in range(1, Z):
                value = value + got[update, s * M + p].astype(f32)
            preds += [value[j * ob : (j + 1) * ob] for j in range(per)]
        if update == 0:
            for load in loads[5:]:
                load.wait()
        mean = functools.reduce(jnp.add, preds) * (1.0 / K)
        seen = obs_ref[...]
        for k in range(K):
            span = pl.ds(k * ob, ob)
            anomaly = preds[k] - mean
            misfit = seen + noise_ref[update, span, :].astype(f32) - preds[k]
            for q in range(samples // 128):
                anomalies[q, span, :] = anomaly[:, q * 128 : (q + 1) * 128]
                misfits[q, span, :] = misfit[:, q * 128 : (q + 1) * 128]
        pieces = [(q, o) for q in range(samples // 128) for o in range(ob)]
        a = jnp.concatenate([anomalies[q, pl.ds(o, K, stride=ob), :] for q, o in pieces], axis=1)
        b = jnp.concatenate([misfits[q, pl.ds(o, K, stride=ob), :] for q, o in pieces], axis=1)
        ab = jnp.concatenate([a, b], axis=0)
        ab_high = ab.astype(bf16)
        ab_low = (ab - ab_high.astype(f32)).astype(bf16)
        a_high = a.astype(bf16).astype(f32)
        left = jnp.concatenate([a_high, a - a_high], axis=0).astype(bf16)
        sums = lax.dot_general(left, ab_high, NT, preferred_element_type=f32)
        sums = sums + lax.dot_general(left, ab_low, NT, preferred_element_type=f32)
        pair[update, c] = jnp.zeros((K, 128), f32)
        pair[update, c, :, 0 : 2 * K] = sums[0:K] + sums[K : 2 * K]
        send(pair.at[update, c], pair.at[update, c], pair_send.at[update], pair_recv.at[update], twin)
        settle(pair.at[update, c], pair_recv.at[update])
        every[update, me] = pair[update, 0] + pair[update, 1]

        for peer in others:
            send(
                every.at[update, me], every.at[update, me],
                every_send.at[update], every_recv.at[update], peer,
            )
        if update == 0:
            decode()
        settle(every.at[update, pl.ds(0, slots - 1)], every_recv.at[update])
        system = jnp.sum(every[update], axis=0) * (1.0 / total)
        system = system + jnp.where(lane == row, RIDGE, 0.0)
        for i in range(K):
            pivot = system[i : i + 1, :]
            pivot = pivot / pivot[:, i : i + 1]
            column = system[:, i : i + 1]
            system = jnp.where(row == i, pivot, system - column * pivot)
        return system

    def columns_of(gain):
        return [
            jnp.sum(jnp.where(lane == K + m * per + j, gain, 0.0), axis=1, keepdims=True)
            for j in range(per)
        ]

    def mixed(columns, top, count):
        span = pl.ds(top, count)
        sums = [full[m, j, span, :] for j in range(per)]
        for k in range(K):
            value = full[k // per, k % per, span, :]
            for j in range(per):
                sums[j] = sums[j] + columns[j][k : k + 1, :] * value
        return sums

    for j in range(per):
        bias[j] = extra_ref[j].astype(f32)[1:2, 0:O].T

    predict(0, own)
    forward()
    first = gain_of(0)
    chosen = columns_of(first)

    def renew(top, count):
        sums = mixed(chosen, top, count)
        for j in range(per):
            fresh[j, pl.ds(top, count), :] = sums[j].astype(bf16)
        return sums

    def chunk(i, carry):
        renew(pl.multiple_of(i * 16, 16), 16)
        return carry

    lax.fori_loop(0, rows // 16, chunk, 0)
    tail = mixed(chosen, F, 16)
    for j in range(per):
        bias[j] = tail[j][1:2, 0:O].T
    send(fresh, other.at[1], w_send.at[1], w_recv.at[1], twin)

    predict(1, fresh)
    second = gain_of(1)

    joint = first + second
    for i in range(K):
        joint = joint + first[:, K + i : K + i + 1] * second[i : i + 1, :]
    chosen_both = columns_of(joint)
    for start, out, size in ((0, new_in_ref, F), (A, new_out_ref, O)):
        def finish(i, carry, start=start, out=out):
            at_row = pl.multiple_of(i * 16, 16)
            sums = mixed(chosen_both, pl.multiple_of(start + i * 16, 16), 16)
            for j in range(per):
                out[j, pl.ds(at_row, 16), :] = sums[j]
            return carry

        lax.fori_loop(0, size // 16, finish, 0)
    sums = mixed(chosen_both, F, 16)
    for j in range(per):
        new_b_in_ref[j : j + 1, :] = sums[j][0:1]
        new_b_out_ref[j : j + 1, :] = sums[j][1:2, 0:O]

    for t in range(1, Z):
        settle(xg.at[0, pl.ds(0, F)], x_send.at[t])
    for t in range(pairs):
        settle(code.at[0], code_send.at[t])
    for t in range(1, pairs):
        settle(code.at[0, first_half], code_send.at[pairs + t])
        settle(code.at[0, second_half], code_send.at[2 * pairs + t])
    for update in range(UPDATES):
        settle(fresh, w_send.at[update])
        settle(got.at[update, pl.ds(0, slots - 1)], piece_send.at[update])
        settle(pair.at[update, 0], pair_send.at[update])
        settle(every.at[update, pl.ds(0, slots - 1)], every_send.at[update])


def place(*refs):
    held, sems = refs[8:12], refs[12]
    loads = [pltpu.make_async_copy(refs[i], held[i], sems.at[i]) for i in range(4)]
    stores = [pltpu.make_async_copy(held[i], refs[4 + i], sems.at[4 + i]) for i in range(4)]
    for load in loads:
        load.start()
    for load, store in zip(loads, stores):
        load.wait()
        store.start()
    for store in stores:
        store.wait()


def on_device(M, Z, inputs, observed, noise, w_in, b_in, w_out, b_out):
    f32, bf16 = jnp.float32, jnp.bfloat16
    per, F, hl = w_in.shape
    O = w_out.shape[1]
    K = per * M
    ob, samples = observed.shape
    rows = F + O + 16
    slots = Z * M
    total = float(O * samples * CORES * Z)
    vmem = pl.BlockSpec(memory_space=pltpu.VMEM)
    dma = pltpu.SemaphoreType.DMA
    hbm = pl.BlockSpec(memory_space=pltpu.HBM)
    results = pl.pallas_call(
        functools.partial(kernel, M, Z, total),
        out_shape=tuple(
            jax.ShapeDtypeStruct(own.shape, f32) for own in (w_in, b_in, w_out, b_out)
        ),
        in_specs=[hbm] * 7,
        out_specs=(vmem,) * 4,
        scratch_shapes=[
            pltpu.VMEM((ob, samples), f32),
            pltpu.VMEM((UPDATES, K * ob, samples), bf16),
            pltpu.VMEM(w_in.shape, f32),
            pltpu.VMEM(b_in.shape, f32),
            pltpu.VMEM(w_out.shape, f32),
            pltpu.VMEM(b_out.shape, f32),
            pltpu.VMEM((per, 16, hl), f32),
            dma((7,)),
            pltpu.VMEM((Z, F + 16, samples), bf16),
            pltpu.VMEM((CORES, per, hl, F + 16), bf16),
            pltpu.VMEM((per, rows, hl), bf16),
            pltpu.VMEM((M, per, rows, hl), bf16),
            pltpu.VMEM((M, per, rows, hl), f32),
            pltpu.VMEM((per, rows, hl), bf16),
            pltpu.VMEM((UPDATES, per, rows, hl), bf16),
            pltpu.VMEM((per, O, 1), f32),
            pltpu.VMEM((UPDATES, Z, M, per * ob, samples), bf16),
            pltpu.VMEM((UPDATES, slots, per * ob, samples), bf16),
            pltpu.VMEM((samples // 128, K * ob, 128), f32),
            pltpu.VMEM((samples // 128, K * ob, 128), f32),
            pltpu.VMEM((UPDATES, CORES, K, 128), f32),
            pltpu.VMEM((UPDATES, slots, K, 128), f32),
            dma((Z,)), dma((Z,)),
            dma((2 * M,)), dma((2 * M,)),
            dma((UPDATES,)), dma((UPDATES,)),
            dma((UPDATES,)), dma((UPDATES,)),
            dma((UPDATES,)), dma((UPDATES,)),
            dma((UPDATES,)), dma((UPDATES,)),
        ],
        compiler_params=pltpu.CompilerParams(
            collective_id=0, has_side_effects=True, vmem_limit_bytes=56 * 1024 * 1024
        ),
        name="inversion",
    )(inputs.T, observed, noise.reshape(UPDATES, K * ob, samples), w_in, b_in, w_out, b_out)
    return pl.pallas_call(
        place,
        out_shape=tuple(jax.ShapeDtypeStruct(own.shape, f32) for own in results),
        in_specs=[hbm] * 4,
        out_specs=(hbm,) * 4,
        scratch_shapes=[pltpu.VMEM(own.shape, f32) for own in results] + [dma((8,))],
        compiler_params=pltpu.CompilerParams(vmem_limit_bytes=56 * 1024 * 1024),
        name="place",
    )(*results)


def solution(mesh):
    placed = (
        P("dp", None),
        P("member", "dp"),
        P(None, None, "member", "dp"),
        P("member", None, "dp"),
        P("member", "dp"),
        P("member", None, "dp"),
        P("member", None),
    )
    return jax.shard_map(
        functools.partial(on_device, mesh.shape["member"], mesh.shape["dp"] // CORES),
        mesh=mesh,
        in_specs=placed,
        out_specs=(
            P("member", None, "dp"),
            P("member", "dp"),
            P("member", None, "dp"),
            P("member", None),
        ),
        check_vma=False,
    )
```

```python
import functools

import jax
import jax.numpy as jnp
from jax import lax
from jax.experimental import pallas as pl
from jax.experimental.pallas import tpu as pltpu
from jax.sharding import PartitionSpec as P

UPDATES = 2
RIDGE = 0.5
CORES = 2
IN_SCALE, BIAS_SCALE, OUT_SCALE = 2.0**15, 2.0**13, 2.0**18
TINY = 2.0**-125
MESH = pl.DeviceIdType.MESH
NT = (((1,), (1,)), ((), ()))


def kernel(
    M, Z, total,
    x_hbm, obs_hbm, noise_hbm, w_in_hbm, b_in_hbm, w_out_hbm, b_out_hbm,
    new_in_ref, new_b_in_ref, new_out_ref, new_b_out_ref,
    obs_ref, noise_ref, w_in_ref, b_in_ref, w_out_ref, b_out_ref, extra_ref, load_sem,
    xg, turned, own, code, full, fresh, other, bias, staged, got, anomalies, misfits, wide, every,
    x_send, x_recv, code_send, code_recv, w_send, w_recv,
    piece_send, piece_recv, every_send, every_recv,
):
    f32, bf16 = jnp.float32, jnp.bfloat16
    m = lax.axis_index("member")
    d = lax.axis_index("dp")
    z, c = d // CORES, d % CORES
    per, F = w_in_ref.shape[0], w_in_ref.shape[1]
    O, hl = w_out_ref.shape[1], w_out_ref.shape[2]
    K = per * M
    ob = O // M
    samples = noise_ref.shape[2]
    rows = own.shape[1]
    A = rows - O
    slots = Z * M
    me = z * M + m
    devices = slots * CORES
    mine = d * M + m
    group = 128 // (2 * K)
    twin = (m, z * CORES + (1 - c))

    members = [lax.rem(m + i, M) for i in range(M)]
    places = [lax.rem(z - i + Z, Z) * CORES + c for i in range(Z)]

    pairs = M // 2
    p_at = [lax.rem(m // 2 + i, pairs) * 2 for i in range(pairs)]
    q = lax.rem(m, 2)

    def send(src, dst, send_sem, recv_sem, target):
        pltpu.make_async_remote_copy(
            src_ref=src, dst_ref=dst, send_sem=send_sem, recv_sem=recv_sem,
            device_id=target, device_id_type=MESH,
        ).start()

    def settle(ref, sem):
        pltpu.make_async_copy(ref, ref, sem).wait()

    loads = [
        pltpu.make_async_copy(src, dst, load_sem.at[i])
        for i, (src, dst) in enumerate((
            (x_hbm, xg.at[z, pl.ds(0, F)]), (w_in_hbm, w_in_ref), (b_in_hbm, b_in_ref),
            (b_out_hbm, b_out_ref), (w_out_hbm, w_out_ref), (obs_hbm, obs_ref), (noise_hbm, noise_ref),
        ))
    ]
    for load in loads:
        load.start()

    barrier = pltpu.get_barrier_semaphore()

    def greet(peer):
        pl.semaphore_signal(barrier, inc=1, device_id=peer, device_id_type=MESH)

    def everyone(act):
        for i in range(M):
            for core in range(CORES):
                if i or core:
                    act((members[i], z * CORES + lax.rem(c + core, CORES)))

        def line(dz, carry):
            place = lax.rem(z + dz, Z) * CORES
            for i in range(M):
                for core in range(CORES):
                    act((members[i], place + core))
            return carry

        lax.fori_loop(1, Z, line, 0, unroll=Z <= 4)

    everyone(greet)

    ones = jnp.where(lax.broadcasted_iota(jnp.int32, (16, samples), 0) == 0, 1.0, 0.0)
    for i in range(Z):
        xg[i, F:A, :] = ones.astype(bf16)
    for load in loads[1:4]:
        load.wait()
    extra_ref[...] = jnp.zeros_like(extra_ref)
    for j in range(per):
        extra_ref[j, 0:1, :] = b_in_ref[j : j + 1, :]
        extra_ref[j, 1:2, 0:O] = b_out_ref[j : j + 1, :]
    loads[4].wait()

    for j in range(per):
        for top, part, scale in (
            (0, w_in_ref[j], IN_SCALE), (F, extra_ref[j], BIAS_SCALE), (A, w_out_ref[j], OUT_SCALE)
        ):
            span = pl.ds(top, part.shape[0])
            own[j, span, :] = part.astype(bf16)
            full[m, j, span, :] = part
            power = part * scale
            for _ in range(3):
                power = power * power
            code[m, j, span, :] = jnp.where(part < 0, -power, power).astype(bf16)
    loads[0].wait()
    pl.semaphore_wait(barrier, devices - 1)

    for t in range(1, Z):
        send(xg.at[z, pl.ds(0, F)], xg.at[z, pl.ds(0, F)], x_send.at[t], x_recv.at[t], (m, places[Z - t]))
    send(own, other.at[0], w_send.at[0], w_recv.at[0], twin)
    def pass_on(src, sem, target):
        send(src, src, code_send.at[sem], code_recv.at[sem], (target, places[0]))

    pass_on(code.at[m], 0, p_at[0] + 1 - q)
    for t in range(1, pairs):
        pass_on(code.at[m], t, p_at[t] + q)

    lane = lax.broadcasted_iota(jnp.int32, (K, 128), 1)
    row = lax.broadcasted_iota(jnp.int32, (K, 128), 0)

    def turn(half, weights):
        for j in range(per):
            turned[half, j] = weights[j, 0:A, :].astype(f32).T.astype(bf16)

    def hidden_part(x, half, weights, j):
        pre = jnp.dot(turned[half, j], x, preferred_element_type=f32)
        hidden = jnp.tanh(pre.astype(bf16))
        return jnp.dot(weights[j, A:rows, :], hidden, preferred_element_type=f32)

    cut = per // 2
    first_half, second_half = pl.ds(0, cut), pl.ds(cut, per - cut)

    def forward():
        for t in range(pairs):
            settle(code.at[0], code_recv.at[t])
        for t in range(1, pairs):
            pass_on(code.at[p_at[0] + 1 - q, first_half], pairs + t, p_at[t] + q)
        for t in range(1, pairs):
            pass_on(code.at[p_at[t] + q, second_half], 2 * pairs + t, p_at[0] + 1 - q)

    def decode():
        for t in range(1, pairs):
            settle(code.at[0, first_half], code_recv.at[pairs + t])
            settle(code.at[0, second_half], code_recv.at[2 * pairs + t])

        def chunk(i, carry):
            slot = lax.rem(m + 1 + i // (per * (rows // 16)), M)
            j = lax.rem(i // (rows // 16), per)
            top = lax.rem(i, rows // 16) * 16
            span = pl.ds(pl.multiple_of(top, 16), 16)
            value = code[slot, j, span, :].astype(f32)
            scale = jnp.where(top < F, 1 / IN_SCALE, jnp.where(top < A, 1 / BIAS_SCALE, 1 / OUT_SCALE))
            size = jnp.abs(value)
            root = jnp.exp2(jnp.log2(jnp.maximum(size, TINY)) * 0.125) * scale
            root = jnp.where(size < TINY, 0.0, root)
            full[slot, j, span, :] = jnp.where(value < 0, -root, root)
            return carry

        lax.fori_loop(0, (M - 1) * per * (rows // 16), chunk, 0, unroll=2)

    def predict(update, own):
        turn(0, own)

        def step(turn_number, carry):
            t = turn_number if update == 0 else lax.rem(turn_number + 1, Z)
            if update == 0:
                @pl.when(t > 0)
                def _():
                    settle(xg.at[0, pl.ds(0, F)], x_recv.at[t])

            target = lax.rem(z - t + Z, Z)
            x = xg[target]
            sums = [hidden_part(x, 0, own, j) for j in range(per)]

            @pl.when(turn_number == 0)
            def _():
                settle(other.at[update], w_recv.at[update])
                turn(1, other.at[update])

            here = jnp.where(t == 0, 1.0, 0.0).astype(f32)
            for j in range(per):
                both = sums[j] + hidden_part(x, 1, other.at[update], j)
                both = (both + here * bias[j]).astype(bf16)
                for p in range(M):
                    staged[update, t, p, j * ob : (j + 1) * ob, :] = both[p * ob : (p + 1) * ob, :]

            def post(to):
                send(
                    staged.at[update, t, to], got.at[update, me],
                    piece_send.at[update], piece_recv.at[update],
                    (to, target * CORES + c),
                )

            for to in members[1:]:
                post(to)

            @pl.when(t > 0)
            def _():
                post(m)

            return carry

        lax.fori_loop(0, Z, step, 0)
        got[update, me] = staged[update, 0, m]

    def turn_rows(value, way):
        result = value
        for g in range(1, group):
            moved = pltpu.roll(value, (way * g * 2 * K) % 128, 1)
            result = jnp.where(lax.rem(row, group) == g, moved, result)
        return result

    def gain_of(update):
        settle(got.at[update, pl.ds(0, slots - 1)], piece_recv.at[update])
        preds = []
        for p in range(M):
            value = got[update, p].astype(f32)
            for s in range(1, Z):
                value = value + got[update, s * M + p].astype(f32)
            preds += [value[j * ob : (j + 1) * ob] for j in range(per)]
        if update == 0:
            for load in loads[5:]:
                load.wait()
        mean = functools.reduce(jnp.add, preds) * (1.0 / K)
        seen = obs_ref[...]
        for k in range(K):
            span = pl.ds(k * ob, ob)
            anomaly = preds[k] - mean
            misfit = seen + noise_ref[update, span, :].astype(f32) - preds[k]
            for q in range(samples // 128):
                anomalies[q, span, :] = anomaly[:, q * 128 : (q + 1) * 128]
                misfits[q, span, :] = misfit[:, q * 128 : (q + 1) * 128]
        pieces = [(q, o) for q in range(samples // 128) for o in range(ob)]
        a = jnp.concatenate([anomalies[q, pl.ds(o, K, stride=ob), :] for q, o in pieces], axis=1)
        b = jnp.concatenate([misfits[q, pl.ds(o, K, stride=ob), :] for q, o in pieces], axis=1)
        ab = jnp.concatenate([a, b], axis=0)
        ab_high = ab.astype(bf16)
        ab_low = (ab - ab_high.astype(f32)).astype(bf16)
        a_high = a.astype(bf16).astype(f32)
        left = jnp.concatenate([a_high, a - a_high], axis=0).astype(bf16)
        sums = lax.dot_general(left, ab_high, NT, preferred_element_type=f32)
        sums = sums + lax.dot_general(left, ab_low, NT, preferred_element_type=f32)
        wide[...] = jnp.zeros((K, 128), f32)
        wide[:, 0 : 2 * K] = sums[0:K] + sums[K : 2 * K]
        spread = turn_rows(wide[...], 1)
        for i in range(K // group):
            every[update, mine, i : i + 1, :] = jnp.sum(
                spread[i * group : (i + 1) * group], axis=0, keepdims=True
            )
        everyone(lambda peer: send(
            every.at[update, mine], every.at[update, mine],
            every_send.at[update], every_recv.at[update], peer,
        ))
        if update == 0:
            decode()
        settle(every.at[update, pl.ds(0, devices - 1)], every_recv.at[update])
        lines = jnp.sum(every[update], axis=0) * (1.0 / total)
        system = jnp.concatenate(
            [jnp.broadcast_to(lines[i : i + 1], (group, 128)) for i in range(K // group)], axis=0
        )
        system = turn_rows(system, -1)
        system = system + jnp.where(lane == row, RIDGE, 0.0)
        for i in range(K):
            pivot = system[i : i + 1, :]
            pivot = pivot / pivot[:, i : i + 1]
            column = system[:, i : i + 1]
            system = jnp.where(row == i, pivot, system - column * pivot)
        return system

    def columns_of(gain):
        return [
            jnp.sum(jnp.where(lane == K + m * per + j, gain, 0.0), axis=1, keepdims=True)
            for j in range(per)
        ]

    def mixed(columns, top, count):
        span = pl.ds(top, count)
        sums = [full[m, j, span, :] for j in range(per)]
        for k in range(K):
            value = full[k // per, k % per, span, :]
            for j in range(per):
                sums[j] = sums[j] + columns[j][k : k + 1, :] * value
        return sums

    for j in range(per):
        bias[j] = extra_ref[j].astype(f32)[1:2, 0:O].T

    predict(0, own)
    forward()
    first = gain_of(0)
    chosen = columns_of(first)

    def renew(top, count):
        sums = mixed(chosen, top, count)
        for j in range(per):
            fresh[j, pl.ds(top, count), :] = sums[j].astype(bf16)
        return sums

    def chunk(i, carry):
        renew(pl.multiple_of(i * 16, 16), 16)
        return carry

    lax.fori_loop(0, rows // 16, chunk, 0)
    tail = mixed(chosen, F, 16)
    for j in range(per):
        bias[j] = tail[j][1:2, 0:O].T
    send(fresh, other.at[1], w_send.at[1], w_recv.at[1], twin)

    predict(1, fresh)
    second = gain_of(1)

    joint = first + second
    for i in range(K):
        joint = joint + first[:, K + i : K + i + 1] * second[i : i + 1, :]
    chosen_both = columns_of(joint)
    for start, out, size in ((0, new_in_ref, F), (A, new_out_ref, O)):
        def finish(i, carry, start=start, out=out):
            at_row = pl.multiple_of(i * 16, 16)
            sums = mixed(chosen_both, pl.multiple_of(start + i * 16, 16), 16)
            for j in range(per):
                out[j, pl.ds(at_row, 16), :] = sums[j]
            return carry

        lax.fori_loop(0, size // 16, finish, 0)
    sums = mixed(chosen_both, F, 16)
    for j in range(per):
        new_b_in_ref[j : j + 1, :] = sums[j][0:1]
        new_b_out_ref[j : j + 1, :] = sums[j][1:2, 0:O]

    for t in range(1, Z):
        settle(xg.at[0, pl.ds(0, F)], x_send.at[t])
    for t in range(pairs):
        settle(code.at[0], code_send.at[t])
    for t in range(1, pairs):
        settle(code.at[0, first_half], code_send.at[pairs + t])
        settle(code.at[0, second_half], code_send.at[2 * pairs + t])
    for update in range(UPDATES):
        settle(fresh, w_send.at[update])
        settle(got.at[update, pl.ds(0, slots - 1)], piece_send.at[update])
        settle(every.at[update, pl.ds(0, devices - 1)], every_send.at[update])


def place(*refs):
    held, sems = refs[8:12], refs[12]
    loads = [pltpu.make_async_copy(refs[i], held[i], sems.at[i]) for i in range(4)]
    stores = [pltpu.make_async_copy(held[i], refs[4 + i], sems.at[4 + i]) for i in range(4)]
    for load in loads:
        load.start()
    for load, store in zip(loads, stores):
        load.wait()
        store.start()
    for store in stores:
        store.wait()


def on_device(M, Z, inputs, observed, noise, w_in, b_in, w_out, b_out):
    f32, bf16 = jnp.float32, jnp.bfloat16
    per, F, hl = w_in.shape
    O = w_out.shape[1]
    K = per * M
    ob, samples = observed.shape
    rows = F + O + 16
    slots = Z * M
    total = float(O * samples * CORES * Z)
    vmem = pl.BlockSpec(memory_space=pltpu.VMEM)
    dma = pltpu.SemaphoreType.DMA
    hbm = pl.BlockSpec(memory_space=pltpu.HBM)
    results = pl.pallas_call(
        functools.partial(kernel, M, Z, total),
        out_shape=tuple(
            jax.ShapeDtypeStruct(own.shape, f32) for own in (w_in, b_in, w_out, b_out)
        ),
        in_specs=[hbm] * 7,
        out_specs=(vmem,) * 4,
        scratch_shapes=[
            pltpu.VMEM((ob, samples), f32),
            pltpu.VMEM((UPDATES, K * ob, samples), bf16),
            pltpu.VMEM(w_in.shape, f32),
            pltpu.VMEM(b_in.shape, f32),
            pltpu.VMEM(w_out.shape, f32),
            pltpu.VMEM(b_out.shape, f32),
            pltpu.VMEM((per, 16, hl), f32),
            dma((7,)),
            pltpu.VMEM((Z, F + 16, samples), bf16),
            pltpu.VMEM((CORES, per, hl, F + 16), bf16),
            pltpu.VMEM((per, rows, hl), bf16),
            pltpu.VMEM((M, per, rows, hl), bf16),
            pltpu.VMEM((M, per, rows, hl), f32),
            pltpu.VMEM((per, rows, hl), bf16),
            pltpu.VMEM((UPDATES, per, rows, hl), bf16),
            pltpu.VMEM((per, O, 1), f32),
            pltpu.VMEM((UPDATES, Z, M, per * ob, samples), bf16),
            pltpu.VMEM((UPDATES, slots, per * ob, samples), bf16),
            pltpu.VMEM((samples // 128, K * ob, 128), f32),
            pltpu.VMEM((samples // 128, K * ob, 128), f32),
            pltpu.VMEM((K, 128), f32),
            pltpu.VMEM((UPDATES, slots * CORES, K * 2 * K // 128, 128), f32),
            dma((Z,)), dma((Z,)),
            dma((2 * M,)), dma((2 * M,)),
            dma((UPDATES,)), dma((UPDATES,)),
            dma((UPDATES,)), dma((UPDATES,)),
            dma((UPDATES,)), dma((UPDATES,)),
        ],
        compiler_params=pltpu.CompilerParams(
            collective_id=0, has_side_effects=True, vmem_limit_bytes=56 * 1024 * 1024
        ),
        name="inversion",
    )(inputs.T, observed, noise.reshape(UPDATES, K * ob, samples), w_in, b_in, w_out, b_out)
    return pl.pallas_call(
        place,
        out_shape=tuple(jax.ShapeDtypeStruct(own.shape, f32) for own in results),
        in_specs=[hbm] * 4,
        out_specs=(hbm,) * 4,
        scratch_shapes=[pltpu.VMEM(own.shape, f32) for own in results] + [dma((8,))],
        compiler_params=pltpu.CompilerParams(vmem_limit_bytes=56 * 1024 * 1024),
        name="place",
    )(*results)


def solution(mesh):
    placed = (
        P("dp", None),
        P("member", "dp"),
        P(None, None, "member", "dp"),
        P("member", None, "dp"),
        P("member", "dp"),
        P("member", None, "dp"),
        P("member", None),
    )
    return jax.shard_map(
        functools.partial(on_device, mesh.shape["member"], mesh.shape["dp"] // CORES),
        mesh=mesh,
        in_specs=placed,
        out_specs=(
            P("member", None, "dp"),
            P("member", "dp"),
            P("member", None, "dp"),
            P("member", None),
        ),
        check_vma=False,
    )
```

```python
import functools

import jax
import jax.numpy as jnp
from jax import lax
from jax.experimental import pallas as pl
from jax.experimental.pallas import tpu as pltpu
from jax.sharding import PartitionSpec as P

UPDATES = 2
RIDGE = 0.5
CORES = 2
IN_SCALE, BIAS_SCALE, OUT_SCALE = 2.0**15, 2.0**13, 2.0**18
TINY = 2.0**-125
MESH = pl.DeviceIdType.MESH
NT = (((1,), (1,)), ((), ()))


def kernel(
    M, Z, total,
    x_hbm, obs_hbm, noise_hbm, w_in_hbm, b_in_hbm, w_out_hbm, b_out_hbm,
    new_in_hbm, new_b_in_hbm, new_out_hbm, new_b_out_hbm,
    obs_ref, noise_ref, w_in_ref, b_in_ref, w_out_ref, b_out_ref, extra_ref, load_sem,
    xg, turned, own, code, full, fresh, other, bias, staged, got, anomalies, misfits, wide, every,
    x_send, x_recv, code_send, code_recv, w_send, w_recv,
    piece_send, piece_recv, every_send, every_recv,
):
    f32, bf16 = jnp.float32, jnp.bfloat16
    m = lax.axis_index("member")
    d = lax.axis_index("dp")
    z, c = d // CORES, d % CORES
    per, F = w_in_ref.shape[0], w_in_ref.shape[1]
    O, hl = w_out_ref.shape[1], w_out_ref.shape[2]
    K = per * M
    ob = O // M
    samples = noise_ref.shape[2]
    rows = own.shape[1]
    A = rows - O
    slots = Z * M
    me = z * M + m
    devices = slots * CORES
    mine = d * M + m
    group = 128 // (2 * K)
    twin = (m, z * CORES + (1 - c))

    members = [lax.rem(m + i, M) for i in range(M)]
    places = [lax.rem(z - i + Z, Z) * CORES + c for i in range(Z)]

    pairs = M // 2
    p_at = [lax.rem(m // 2 + i, pairs) * 2 for i in range(pairs)]
    q = lax.rem(m, 2)

    def send(src, dst, send_sem, recv_sem, target):
        pltpu.make_async_remote_copy(
            src_ref=src, dst_ref=dst, send_sem=send_sem, recv_sem=recv_sem,
            device_id=target, device_id_type=MESH,
        ).start()

    def settle(ref, sem):
        pltpu.make_async_copy(ref, ref, sem).wait()

    loads = [
        pltpu.make_async_copy(src, dst, load_sem.at[i])
        for i, (src, dst) in enumerate((
            (x_hbm, xg.at[z, pl.ds(0, F)]), (w_in_hbm, w_in_ref), (b_in_hbm, b_in_ref),
            (b_out_hbm, b_out_ref), (w_out_hbm, w_out_ref), (obs_hbm, obs_ref), (noise_hbm, noise_ref),
        ))
    ]
    for load in loads:
        load.start()

    barrier = pltpu.get_barrier_semaphore()

    def greet(peer):
        pl.semaphore_signal(barrier, inc=1, device_id=peer, device_id_type=MESH)

    def everyone(act):
        for i in range(M):
            for core in range(CORES):
                if i or core:
                    act((members[i], z * CORES + lax.rem(c + core, CORES)))

        def line(dz, carry):
            place = lax.rem(z + dz, Z) * CORES
            for i in range(M):
                for core in range(CORES):
                    act((members[i], place + core))
            return carry

        lax.fori_loop(1, Z, line, 0, unroll=Z <= 4)

    everyone(greet)

    ones = jnp.where(lax.broadcasted_iota(jnp.int32, (16, samples), 0) == 0, 1.0, 0.0)
    for i in range(Z):
        xg[i, F:A, :] = ones.astype(bf16)
    for load in loads[1:4]:
        load.wait()
    extra_ref[...] = jnp.zeros_like(extra_ref)
    for j in range(per):
        extra_ref[j, 0:1, :] = b_in_ref[j : j + 1, :]
        extra_ref[j, 1:2, 0:O] = b_out_ref[j : j + 1, :]
    loads[4].wait()

    for j in range(per):
        for top, part, scale in (
            (0, w_in_ref[j], IN_SCALE), (F, extra_ref[j], BIAS_SCALE), (A, w_out_ref[j], OUT_SCALE)
        ):
            span = pl.ds(top, part.shape[0])
            own[j, span, :] = part.astype(bf16)
            full[m, j, span, :] = part
            power = part * scale
            for _ in range(3):
                power = power * power
            code[m, j, span, :] = jnp.where(part < 0, -power, power).astype(bf16)
    loads[0].wait()
    pl.semaphore_wait(barrier, devices - 1)

    for t in range(1, Z):
        send(xg.at[z, pl.ds(0, F)], xg.at[z, pl.ds(0, F)], x_send.at[t], x_recv.at[t], (m, places[Z - t]))
    send(own, other.at[0], w_send.at[0], w_recv.at[0], twin)
    def pass_on(src, sem, target):
        send(src, src, code_send.at[sem], code_recv.at[sem], (target, places[0]))

    pass_on(code.at[m], 0, p_at[0] + 1 - q)
    for t in range(1, pairs):
        pass_on(code.at[m], t, p_at[t] + q)

    lane = lax.broadcasted_iota(jnp.int32, (K, 128), 1)
    row = lax.broadcasted_iota(jnp.int32, (K, 128), 0)

    def turn(half, weights):
        for j in range(per):
            turned[half, j] = weights[j, 0:A, :].astype(f32).T.astype(bf16)

    def hidden_part(x, half, weights, j):
        pre = jnp.dot(turned[half, j], x, preferred_element_type=f32)
        hidden = jnp.tanh(pre.astype(bf16))
        return jnp.dot(weights[j, A:rows, :], hidden, preferred_element_type=f32)

    cut = per // 2
    first_half, second_half = pl.ds(0, cut), pl.ds(cut, per - cut)

    def forward():
        for t in range(pairs):
            settle(code.at[0], code_recv.at[t])
        for t in range(1, pairs):
            pass_on(code.at[p_at[0] + 1 - q, first_half], pairs + t, p_at[t] + q)
        for t in range(1, pairs):
            pass_on(code.at[p_at[t] + q, second_half], 2 * pairs + t, p_at[0] + 1 - q)

    def decode():
        for t in range(1, pairs):
            settle(code.at[0, first_half], code_recv.at[pairs + t])
            settle(code.at[0, second_half], code_recv.at[2 * pairs + t])

        def chunk(i, carry):
            slot = lax.rem(m + 1 + i // (per * (rows // 16)), M)
            j = lax.rem(i // (rows // 16), per)
            top = lax.rem(i, rows // 16) * 16
            span = pl.ds(pl.multiple_of(top, 16), 16)
            value = code[slot, j, span, :].astype(f32)
            scale = jnp.where(top < F, 1 / IN_SCALE, jnp.where(top < A, 1 / BIAS_SCALE, 1 / OUT_SCALE))
            size = jnp.abs(value)
            root = jnp.exp2(jnp.log2(jnp.maximum(size, TINY)) * 0.125) * scale
            root = jnp.where(size < TINY, 0.0, root)
            full[slot, j, span, :] = jnp.where(value < 0, -root, root)
            return carry

        lax.fori_loop(0, (M - 1) * per * (rows // 16), chunk, 0, unroll=2)

    def predict(update, own):
        turn(0, own)

        def step(turn_number):
            t = turn_number if update == 0 else lax.rem(turn_number + 1, Z)
            peeled = isinstance(turn_number, int)
            if update == 0 and not peeled:
                settle(xg.at[0, pl.ds(0, F)], x_recv.at[t])

            target = lax.rem(z - t + Z, Z)
            x = xg[target]
            sums = [hidden_part(x, 0, own, j) for j in range(per)]

            if peeled:
                settle(other.at[update], w_recv.at[update])
                turn(1, other.at[update])

            here = jnp.where(t == 0, 1.0, 0.0).astype(f32)
            for j in range(per):
                both = sums[j] + hidden_part(x, 1, other.at[update], j)
                both = (both + here * bias[j]).astype(bf16)
                for p in range(M):
                    staged[update, t, p, j * ob : (j + 1) * ob, :] = both[p * ob : (p + 1) * ob, :]

            def post(to):
                send(
                    staged.at[update, t, to], got.at[update, me],
                    piece_send.at[update], piece_recv.at[update],
                    (to, target * CORES + c),
                )

            for to in members[1:]:
                post(to)

            @pl.when(t > 0)
            def _():
                post(m)

        def block(i, carry):
            step(i)
            return carry

        step(0)
        lax.fori_loop(1, Z, block, 0)
        got[update, me] = staged[update, 0, m]

    def turn_rows(value, way):
        result = value
        for g in range(1, group):
            moved = pltpu.roll(value, (way * g * 2 * K) % 128, 1)
            result = jnp.where(lax.rem(row, group) == g, moved, result)
        return result

    def gain_of(update):
        settle(got.at[update, pl.ds(0, slots - 1)], piece_recv.at[update])
        preds = []
        for p in range(M):
            value = got[update, p].astype(f32)
            for s in range(1, Z):
                value = value + got[update, s * M + p].astype(f32)
            preds += [value[j * ob : (j + 1) * ob] for j in range(per)]
        if update == 0:
            for load in loads[5:]:
                load.wait()
        mean = functools.reduce(jnp.add, preds) * (1.0 / K)
        seen = obs_ref[...]
        for k in range(K):
            span = pl.ds(k * ob, ob)
            anomaly = preds[k] - mean
            misfit = seen + noise_ref[update, span, :].astype(f32) - preds[k]
            for q in range(samples // 128):
                anomalies[q, span, :] = anomaly[:, q * 128 : (q + 1) * 128]
                misfits[q, span, :] = misfit[:, q * 128 : (q + 1) * 128]
        pieces = [(q, o) for q in range(samples // 128) for o in range(ob)]
        a = jnp.concatenate([anomalies[q, pl.ds(o, K, stride=ob), :] for q, o in pieces], axis=1)
        b = jnp.concatenate([misfits[q, pl.ds(o, K, stride=ob), :] for q, o in pieces], axis=1)
        ab = jnp.concatenate([a, b], axis=0)
        ab_high = ab.astype(bf16)
        ab_low = (ab - ab_high.astype(f32)).astype(bf16)
        a_high = a.astype(bf16).astype(f32)
        left = jnp.concatenate([a_high, a - a_high], axis=0).astype(bf16)
        sums = lax.dot_general(left, ab_high, NT, preferred_element_type=f32)
        sums = sums + lax.dot_general(left, ab_low, NT, preferred_element_type=f32)
        wide[...] = jnp.zeros((K, 128), f32)
        wide[:, 0 : 2 * K] = sums[0:K] + sums[K : 2 * K]
        spread = turn_rows(wide[...], 1)
        for i in range(K // group):
            every[update, mine, i : i + 1, :] = jnp.sum(
                spread[i * group : (i + 1) * group], axis=0, keepdims=True
            )
        everyone(lambda peer: send(
            every.at[update, mine], every.at[update, mine],
            every_send.at[update], every_recv.at[update], peer,
        ))
        if update == 0:
            decode()
        settle(every.at[update, pl.ds(0, devices - 1)], every_recv.at[update])
        lines = jnp.sum(every[update], axis=0) * (1.0 / total)
        system = jnp.concatenate(
            [jnp.broadcast_to(lines[i : i + 1], (group, 128)) for i in range(K // group)], axis=0
        )
        system = turn_rows(system, -1)
        system = system + jnp.where(lane == row, RIDGE, 0.0)
        for i in range(K):
            pivot = system[i : i + 1, :]
            pivot = pivot / pivot[:, i : i + 1]
            column = system[:, i : i + 1]
            system = jnp.where(row == i, pivot, system - column * pivot)
        return system

    def columns_of(gain):
        return [
            jnp.sum(jnp.where(lane == K + m * per + j, gain, 0.0), axis=1, keepdims=True)
            for j in range(per)
        ]

    def mixed(columns, top, count):
        span = pl.ds(top, count)
        sums = [full[m, j, span, :] for j in range(per)]
        for k in range(K):
            value = full[k // per, k % per, span, :]
            for j in range(per):
                sums[j] = sums[j] + columns[j][k : k + 1, :] * value
        return sums

    for j in range(per):
        bias[j] = extra_ref[j].astype(f32)[1:2, 0:O].T

    predict(0, own)
    forward()
    first = gain_of(0)
    chosen = columns_of(first)

    def renew(top, count):
        sums = mixed(chosen, top, count)
        for j in range(per):
            fresh[j, pl.ds(top, count), :] = sums[j].astype(bf16)
        return sums

    def chunk(i, carry):
        renew(pl.multiple_of(i * 16, 16), 16)
        return carry

    lax.fori_loop(0, rows // 16, chunk, 0)
    tail = mixed(chosen, F, 16)
    for j in range(per):
        bias[j] = tail[j][1:2, 0:O].T
    send(fresh, other.at[1], w_send.at[1], w_recv.at[1], twin)

    predict(1, fresh)
    second = gain_of(1)

    joint = first + second
    for i in range(K):
        joint = joint + first[:, K + i : K + i + 1] * second[i : i + 1, :]
    chosen_both = columns_of(joint)
    exits = [
        pltpu.make_async_copy(src, dst, load_sem.at[n])
        for n, (src, dst) in enumerate((
            (w_in_ref, new_in_hbm), (w_out_ref, new_out_hbm),
            (b_in_ref, new_b_in_hbm), (b_out_ref, new_b_out_hbm),
        ))
    ]

    def leave(ref):
        exits[0 if ref is w_in_ref else 1].start()

    for start, out, size in ((0, w_in_ref, F), (A, w_out_ref, O)):
        def finish(i, carry, start=start, out=out):
            at_row = pl.multiple_of(i * 16, 16)
            sums = mixed(chosen_both, pl.multiple_of(start + i * 16, 16), 16)
            for j in range(per):
                out[j, pl.ds(at_row, 16), :] = sums[j]
            return carry

        lax.fori_loop(0, size // 16, finish, 0)
        leave(out)
    sums = mixed(chosen_both, F, 16)
    for j in range(per):
        b_in_ref[j : j + 1, :] = sums[j][0:1]
        b_out_ref[j : j + 1, :] = sums[j][1:2, 0:O]
    exits[2].start()
    exits[3].start()

    for leaving in exits:
        leaving.wait()
    for t in range(1, Z):
        settle(xg.at[0, pl.ds(0, F)], x_send.at[t])
    for t in range(pairs):
        settle(code.at[0], code_send.at[t])
    for t in range(1, pairs):
        settle(code.at[0, first_half], code_send.at[pairs + t])
        settle(code.at[0, second_half], code_send.at[2 * pairs + t])
    for update in range(UPDATES):
        settle(fresh, w_send.at[update])
        settle(got.at[update, pl.ds(0, slots - 1)], piece_send.at[update])
        settle(every.at[update, pl.ds(0, devices - 1)], every_send.at[update])


def place(*refs):
    held, sems = refs[8:12], refs[12]
    loads = [pltpu.make_async_copy(refs[i], held[i], sems.at[i]) for i in range(4)]
    stores = [pltpu.make_async_copy(held[i], refs[4 + i], sems.at[4 + i]) for i in range(4)]
    for load in loads:
        load.start()
    for load, store in zip(loads, stores):
        load.wait()
        store.start()
    for store in stores:
        store.wait()


def on_device(M, Z, inputs, observed, noise, w_in, b_in, w_out, b_out):
    f32, bf16 = jnp.float32, jnp.bfloat16
    per, F, hl = w_in.shape
    O = w_out.shape[1]
    K = per * M
    ob, samples = observed.shape
    rows = F + O + 16
    slots = Z * M
    total = float(O * samples * CORES * Z)
    dma = pltpu.SemaphoreType.DMA
    hbm = pl.BlockSpec(memory_space=pltpu.HBM)
    results = pl.pallas_call(
        functools.partial(kernel, M, Z, total),
        out_shape=tuple(
            jax.ShapeDtypeStruct(own.shape, f32) for own in (w_in, b_in, w_out, b_out)
        ),
        in_specs=[hbm] * 7,
        out_specs=(hbm,) * 4,
        scratch_shapes=[
            pltpu.VMEM((ob, samples), f32),
            pltpu.VMEM((UPDATES, K * ob, samples), bf16),
            pltpu.VMEM(w_in.shape, f32),
            pltpu.VMEM(b_in.shape, f32),
            pltpu.VMEM(w_out.shape, f32),
            pltpu.VMEM(b_out.shape, f32),
            pltpu.VMEM((per, 16, hl), f32),
            dma((7,)),
            pltpu.VMEM((Z, F + 16, samples), bf16),
            pltpu.VMEM((CORES, per, hl, F + 16), bf16),
            pltpu.VMEM((per, rows, hl), bf16),
            pltpu.VMEM((M, per, rows, hl), bf16),
            pltpu.VMEM((M, per, rows, hl), f32),
            pltpu.VMEM((per, rows, hl), bf16),
            pltpu.VMEM((UPDATES, per, rows, hl), bf16),
            pltpu.VMEM((per, O, 1), f32),
            pltpu.VMEM((UPDATES, Z, M, per * ob, samples), bf16),
            pltpu.VMEM((UPDATES, slots, per * ob, samples), bf16),
            pltpu.VMEM((samples // 128, K * ob, 128), f32),
            pltpu.VMEM((samples // 128, K * ob, 128), f32),
            pltpu.VMEM((K, 128), f32),
            pltpu.VMEM((UPDATES, slots * CORES, K * 2 * K // 128, 128), f32),
            dma((Z,)), dma((Z,)),
            dma((2 * M,)), dma((2 * M,)),
            dma((UPDATES,)), dma((UPDATES,)),
            dma((UPDATES,)), dma((UPDATES,)),
            dma((UPDATES,)), dma((UPDATES,)),
        ],
        compiler_params=pltpu.CompilerParams(
            collective_id=0, has_side_effects=True, vmem_limit_bytes=56 * 1024 * 1024
        ),
        name="inversion",
    )(inputs.T, observed, noise.reshape(UPDATES, K * ob, samples), w_in, b_in, w_out, b_out)
    return pl.pallas_call(
        place,
        out_shape=tuple(jax.ShapeDtypeStruct(own.shape, f32) for own in results),
        in_specs=[hbm] * 4,
        out_specs=(hbm,) * 4,
        scratch_shapes=[pltpu.VMEM(own.shape, f32) for own in results] + [dma((8,))],
        compiler_params=pltpu.CompilerParams(vmem_limit_bytes=56 * 1024 * 1024),
        name="place",
    )(*results)


def solution(mesh):
    placed = (
        P("dp", None),
        P("member", "dp"),
        P(None, None, "member", "dp"),
        P("member", None, "dp"),
        P("member", "dp"),
        P("member", None, "dp"),
        P("member", None),
    )
    return jax.shard_map(
        functools.partial(on_device, mesh.shape["member"], mesh.shape["dp"] // CORES),
        mesh=mesh,
        in_specs=placed,
        out_specs=(
            P("member", None, "dp"),
            P("member", "dp"),
            P("member", None, "dp"),
            P("member", None),
        ),
        check_vma=False,
    )
```

```python
import functools

import jax
import jax.numpy as jnp
from jax import lax
from jax.experimental import pallas as pl
from jax.experimental.pallas import tpu as pltpu
from jax.sharding import PartitionSpec as P

UPDATES = 2
RIDGE = 0.5
CORES = 2
IN_SCALE, BIAS_SCALE, OUT_SCALE = 2.0**15, 2.0**13, 2.0**18
TINY = 2.0**-125
MESH = pl.DeviceIdType.MESH
NT = (((1,), (1,)), ((), ()))


def kernel(
    M, Z, total,
    x_hbm, obs_hbm, noise_hbm, w_in_hbm, b_in_hbm, w_out_hbm, b_out_hbm,
    new_in_hbm, new_b_in_hbm, new_out_hbm, new_b_out_hbm,
    obs_ref, noise_ref, w_in_ref, b_in_ref, w_out_ref, b_out_ref, extra_ref, load_sem,
    xg, turned, own, code, full, fresh, other, bias, staged, got, anomalies, misfits, wide, every,
    x_send, x_recv, code_send, code_recv, w_send, w_recv,
    piece_send, piece_recv, every_send, every_recv,
):
    f32, bf16 = jnp.float32, jnp.bfloat16
    m = lax.axis_index("member")
    d = lax.axis_index("dp")
    z, c = d // CORES, d % CORES
    per, F = w_in_ref.shape[0], w_in_ref.shape[1]
    O, hl = w_out_ref.shape[1], w_out_ref.shape[2]
    K = per * M
    ob = O // M
    samples = noise_ref.shape[2]
    rows = own.shape[1]
    A = rows - O
    slots = Z * M
    me = z * M + m
    devices = slots * CORES
    mine = d * M + m
    group = 128 // (2 * K)
    twin = (m, z * CORES + (1 - c))

    members = [lax.rem(m + i, M) for i in range(M)]
    places = [lax.rem(z - i + Z, Z) * CORES + c for i in range(Z)]

    pairs = M // 2
    p_at = [lax.rem(m // 2 + i, pairs) * 2 for i in range(pairs)]
    q = lax.rem(m, 2)

    def send(src, dst, send_sem, recv_sem, target):
        pltpu.make_async_remote_copy(
            src_ref=src, dst_ref=dst, send_sem=send_sem, recv_sem=recv_sem,
            device_id=target, device_id_type=MESH,
        ).start()

    def settle(ref, sem):
        pltpu.make_async_copy(ref, ref, sem).wait()

    loads = [
        pltpu.make_async_copy(src, dst, load_sem.at[i])
        for i, (src, dst) in enumerate((
            (x_hbm, xg.at[z, pl.ds(0, F)]), (w_in_hbm, w_in_ref), (b_in_hbm, b_in_ref),
            (b_out_hbm, b_out_ref), (w_out_hbm, w_out_ref), (obs_hbm, obs_ref), (noise_hbm, noise_ref),
        ))
    ]
    for load in loads:
        load.start()

    barrier = pltpu.get_barrier_semaphore()

    def greet(peer):
        pl.semaphore_signal(barrier, inc=1, device_id=peer, device_id_type=MESH)

    def everyone(act):
        for i in range(M):
            for core in range(CORES):
                if i or core:
                    act((members[i], z * CORES + lax.rem(c + core, CORES)))

        def line(dz, carry):
            place = lax.rem(z + dz, Z) * CORES
            for i in range(M):
                for core in range(CORES):
                    act((members[i], place + core))
            return carry

        lax.fori_loop(1, Z, line, 0, unroll=Z <= 4)

    everyone(greet)

    ones = jnp.where(lax.broadcasted_iota(jnp.int32, (16, samples), 0) == 0, 1.0, 0.0)
    for i in range(Z):
        xg[i, F:A, :] = ones.astype(bf16)
    for load in loads[1:4]:
        load.wait()
    extra_ref[...] = jnp.zeros_like(extra_ref)
    for j in range(per):
        extra_ref[j, 0:1, :] = b_in_ref[j : j + 1, :]
        extra_ref[j, 1:2, 0:O] = b_out_ref[j : j + 1, :]
    loads[4].wait()

    for j in range(per):
        for top, part, scale in (
            (0, w_in_ref[j], IN_SCALE), (F, extra_ref[j], BIAS_SCALE), (A, w_out_ref[j], OUT_SCALE)
        ):
            span = pl.ds(top, part.shape[0])
            own[j, span, :] = part.astype(bf16)
            full[m, j, span, :] = part
            power = part * scale
            for _ in range(3):
                power = power * power
            code[m, j, span, :] = jnp.where(part < 0, -power, power).astype(bf16)
    loads[0].wait()
    pl.semaphore_wait(barrier, devices - 1)

    for t in range(1, Z):
        send(xg.at[z, pl.ds(0, F)], xg.at[z, pl.ds(0, F)], x_send.at[t], x_recv.at[t], (m, places[Z - t]))
    send(own, other.at[0], w_send.at[0], w_recv.at[0], twin)
    def pass_on(src, sem, target):
        send(src, src, code_send.at[sem], code_recv.at[sem], (target, places[0]))

    cut = per // 2
    first_half, second_half = pl.ds(0, cut), pl.ds(cut, per - cut)
    pass_on(code.at[m, first_half], 0, p_at[0] + 1 - q)
    for t in range(1, pairs):
        pass_on(code.at[m, second_half], t, p_at[t] + q)
    pass_on(code.at[m, second_half], pairs, p_at[0] + 1 - q)
    for t in range(1, pairs):
        pass_on(code.at[m, first_half], pairs + t, p_at[t] + q)

    lane = lax.broadcasted_iota(jnp.int32, (K, 128), 1)
    row = lax.broadcasted_iota(jnp.int32, (K, 128), 0)

    def turn(half, weights):
        for j in range(per):
            turned[half, j] = weights[j, 0:A, :].astype(f32).T.astype(bf16)

    def hidden_part(x, half, weights, j):
        pre = jnp.dot(turned[half, j], x, preferred_element_type=f32)
        hidden = jnp.tanh(pre.astype(bf16))
        return jnp.dot(weights[j, A:rows, :], hidden, preferred_element_type=f32)

    def forward():
        for t in range(pairs):
            settle(code.at[0, second_half if t else first_half], code_recv.at[t])
        for t in range(1, pairs):
            pass_on(code.at[p_at[0] + 1 - q, first_half], 2 * pairs + t, p_at[t] + q)
        for t in range(1, pairs):
            pass_on(code.at[p_at[t] + q, second_half], 3 * pairs + t, p_at[0] + 1 - q)

    def decode():
        for t in range(pairs):
            settle(code.at[0, first_half if t else second_half], code_recv.at[pairs + t])
        for t in range(1, pairs):
            settle(code.at[0, first_half], code_recv.at[2 * pairs + t])
            settle(code.at[0, second_half], code_recv.at[3 * pairs + t])

        def chunk(i, carry):
            slot = lax.rem(m + 1 + i // (per * (rows // 16)), M)
            j = lax.rem(i // (rows // 16), per)
            top = lax.rem(i, rows // 16) * 16
            span = pl.ds(pl.multiple_of(top, 16), 16)
            value = code[slot, j, span, :].astype(f32)
            scale = jnp.where(top < F, 1 / IN_SCALE, jnp.where(top < A, 1 / BIAS_SCALE, 1 / OUT_SCALE))
            size = jnp.abs(value)
            root = jnp.exp2(jnp.log2(jnp.maximum(size, TINY)) * 0.125) * scale
            root = jnp.where(size < TINY, 0.0, root)
            full[slot, j, span, :] = jnp.where(value < 0, -root, root)
            return carry

        lax.fori_loop(0, (M - 1) * per * (rows // 16), chunk, 0, unroll=2)

    def predict(update, own):
        turn(0, own)

        def step(turn_number):
            t = turn_number if update == 0 else lax.rem(turn_number + 1, Z)
            peeled = isinstance(turn_number, int)
            if update == 0 and not peeled:
                settle(xg.at[0, pl.ds(0, F)], x_recv.at[t])

            target = lax.rem(z - t + Z, Z)
            x = xg[target]
            sums = [hidden_part(x, 0, own, j) for j in range(per)]

            if peeled:
                settle(other.at[update], w_recv.at[update])
                turn(1, other.at[update])

            here = jnp.where(t == 0, 1.0, 0.0).astype(f32)
            for j in range(per):
                both = sums[j] + hidden_part(x, 1, other.at[update], j)
                both = (both + here * bias[j]).astype(bf16)
                for p in range(M):
                    staged[update, t, p, j * ob : (j + 1) * ob, :] = both[p * ob : (p + 1) * ob, :]

            def post(to):
                send(
                    staged.at[update, t, to], got.at[update, me],
                    piece_send.at[update], piece_recv.at[update],
                    (to, target * CORES + c),
                )

            for to in members[1:]:
                post(to)

            @pl.when(t > 0)
            def _():
                post(m)

        def block(i, carry):
            step(i)
            return carry

        step(0)
        lax.fori_loop(1, Z, block, 0)
        got[update, me] = staged[update, 0, m]

    def turn_rows(value, way):
        result = value
        for g in range(1, group):
            moved = pltpu.roll(value, (way * g * 2 * K) % 128, 1)
            result = jnp.where(lax.rem(row, group) == g, moved, result)
        return result

    def gain_of(update):
        settle(got.at[update, pl.ds(0, slots - 1)], piece_recv.at[update])
        preds = []
        for p in range(M):
            value = got[update, p].astype(f32)
            for s in range(1, Z):
                value = value + got[update, s * M + p].astype(f32)
            preds += [value[j * ob : (j + 1) * ob] for j in range(per)]
        if update == 0:
            for load in loads[5:]:
                load.wait()
        mean = functools.reduce(jnp.add, preds) * (1.0 / K)
        seen = obs_ref[...]
        for k in range(K):
            span = pl.ds(k * ob, ob)
            anomaly = preds[k] - mean
            misfit = seen + noise_ref[update, span, :].astype(f32) - preds[k]
            for q in range(samples // 128):
                anomalies[q, span, :] = anomaly[:, q * 128 : (q + 1) * 128]
                misfits[q, span, :] = misfit[:, q * 128 : (q + 1) * 128]
        pieces = [(q, o) for q in range(samples // 128) for o in range(ob)]
        a = jnp.concatenate([anomalies[q, pl.ds(o, K, stride=ob), :] for q, o in pieces], axis=1)
        b = jnp.concatenate([misfits[q, pl.ds(o, K, stride=ob), :] for q, o in pieces], axis=1)
        ab = jnp.concatenate([a, b], axis=0)
        ab_high = ab.astype(bf16)
        ab_low = (ab - ab_high.astype(f32)).astype(bf16)
        a_high = a.astype(bf16).astype(f32)
        left = jnp.concatenate([a_high, a - a_high], axis=0).astype(bf16)
        sums = lax.dot_general(left, ab_high, NT, preferred_element_type=f32)
        sums = sums + lax.dot_general(left, ab_low, NT, preferred_element_type=f32)
        wide[...] = jnp.zeros((K, 128), f32)
        wide[:, 0 : 2 * K] = sums[0:K] + sums[K : 2 * K]
        spread = turn_rows(wide[...], 1)
        for i in range(K // group):
            every[update, mine, i : i + 1, :] = jnp.sum(
                spread[i * group : (i + 1) * group], axis=0, keepdims=True
            )
        everyone(lambda peer: send(
            every.at[update, mine], every.at[update, mine],
            every_send.at[update], every_recv.at[update], peer,
        ))
        if update == 0:
            decode()
        settle(every.at[update, pl.ds(0, devices - 1)], every_recv.at[update])
        lines = jnp.sum(every[update], axis=0) * (1.0 / total)
        system = jnp.concatenate(
            [jnp.broadcast_to(lines[i : i + 1], (group, 128)) for i in range(K // group)], axis=0
        )
        system = turn_rows(system, -1)
        system = system + jnp.where(lane == row, RIDGE, 0.0)
        for i in range(K):
            pivot = system[i : i + 1, :]
            pivot = pivot / pivot[:, i : i + 1]
            column = system[:, i : i + 1]
            system = jnp.where(row == i, pivot, system - column * pivot)
        return system

    def columns_of(gain):
        return [
            jnp.sum(jnp.where(lane == K + m * per + j, gain, 0.0), axis=1, keepdims=True)
            for j in range(per)
        ]

    def mixed(columns, top, count):
        span = pl.ds(top, count)
        sums = [full[m, j, span, :] for j in range(per)]
        for k in range(K):
            value = full[k // per, k % per, span, :]
            for j in range(per):
                sums[j] = sums[j] + columns[j][k : k + 1, :] * value
        return sums

    for j in range(per):
        bias[j] = extra_ref[j].astype(f32)[1:2, 0:O].T

    predict(0, own)
    forward()
    first = gain_of(0)
    chosen = columns_of(first)

    def renew(top, count):
        sums = mixed(chosen, top, count)
        for j in range(per):
            fresh[j, pl.ds(top, count), :] = sums[j].astype(bf16)
        return sums

    def chunk(i, carry):
        renew(pl.multiple_of(i * 16, 16), 16)
        return carry

    lax.fori_loop(0, rows // 16, chunk, 0)
    tail = mixed(chosen, F, 16)
    for j in range(per):
        bias[j] = tail[j][1:2, 0:O].T
    send(fresh, other.at[1], w_send.at[1], w_recv.at[1], twin)

    predict(1, fresh)
    second = gain_of(1)

    joint = first + second
    for i in range(K):
        joint = joint + first[:, K + i : K + i + 1] * second[i : i + 1, :]
    chosen_both = columns_of(joint)
    exits = [
        pltpu.make_async_copy(src, dst, load_sem.at[n])
        for n, (src, dst) in enumerate((
            (w_in_ref, new_in_hbm), (w_out_ref, new_out_hbm),
            (b_in_ref, new_b_in_hbm), (b_out_ref, new_b_out_hbm),
        ))
    ]

    def leave(ref):
        exits[0 if ref is w_in_ref else 1].start()

    for start, out, size in ((0, w_in_ref, F), (A, w_out_ref, O)):
        def finish(i, carry, start=start, out=out):
            at_row = pl.multiple_of(i * 16, 16)
            sums = mixed(chosen_both, pl.multiple_of(start + i * 16, 16), 16)
            for j in range(per):
                out[j, pl.ds(at_row, 16), :] = sums[j]
            return carry

        lax.fori_loop(0, size // 16, finish, 0)
        leave(out)
    sums = mixed(chosen_both, F, 16)
    for j in range(per):
        b_in_ref[j : j + 1, :] = sums[j][0:1]
        b_out_ref[j : j + 1, :] = sums[j][1:2, 0:O]
    exits[2].start()
    exits[3].start()

    for leaving in exits:
        leaving.wait()
    for t in range(1, Z):
        settle(xg.at[0, pl.ds(0, F)], x_send.at[t])
    for t in range(pairs):
        settle(code.at[0, second_half if t else first_half], code_send.at[t])
        settle(code.at[0, first_half if t else second_half], code_send.at[pairs + t])
    for t in range(1, pairs):
        settle(code.at[0, first_half], code_send.at[2 * pairs + t])
        settle(code.at[0, second_half], code_send.at[3 * pairs + t])
    for update in range(UPDATES):
        settle(fresh, w_send.at[update])
        settle(got.at[update, pl.ds(0, slots - 1)], piece_send.at[update])
        settle(every.at[update, pl.ds(0, devices - 1)], every_send.at[update])


def place(*refs):
    held, sems = refs[8:12], refs[12]
    loads = [pltpu.make_async_copy(refs[i], held[i], sems.at[i]) for i in range(4)]
    stores = [pltpu.make_async_copy(held[i], refs[4 + i], sems.at[4 + i]) for i in range(4)]
    for load in loads:
        load.start()
    for load, store in zip(loads, stores):
        load.wait()
        store.start()
    for store in stores:
        store.wait()


def on_device(M, Z, inputs, observed, noise, w_in, b_in, w_out, b_out):
    f32, bf16 = jnp.float32, jnp.bfloat16
    per, F, hl = w_in.shape
    O = w_out.shape[1]
    K = per * M
    ob, samples = observed.shape
    rows = F + O + 16
    slots = Z * M
    total = float(O * samples * CORES * Z)
    dma = pltpu.SemaphoreType.DMA
    hbm = pl.BlockSpec(memory_space=pltpu.HBM)
    results = pl.pallas_call(
        functools.partial(kernel, M, Z, total),
        out_shape=tuple(
            jax.ShapeDtypeStruct(own.shape, f32) for own in (w_in, b_in, w_out, b_out)
        ),
        in_specs=[hbm] * 7,
        out_specs=(hbm,) * 4,
        scratch_shapes=[
            pltpu.VMEM((ob, samples), f32),
            pltpu.VMEM((UPDATES, K * ob, samples), bf16),
            pltpu.VMEM(w_in.shape, f32),
            pltpu.VMEM(b_in.shape, f32),
            pltpu.VMEM(w_out.shape, f32),
            pltpu.VMEM(b_out.shape, f32),
            pltpu.VMEM((per, 16, hl), f32),
            dma((7,)),
            pltpu.VMEM((Z, F + 16, samples), bf16),
            pltpu.VMEM((CORES, per, hl, F + 16), bf16),
            pltpu.VMEM((per, rows, hl), bf16),
            pltpu.VMEM((M, per, rows, hl), bf16),
            pltpu.VMEM((M, per, rows, hl), f32),
            pltpu.VMEM((per, rows, hl), bf16),
            pltpu.VMEM((UPDATES, per, rows, hl), bf16),
            pltpu.VMEM((per, O, 1), f32),
            pltpu.VMEM((UPDATES, Z, M, per * ob, samples), bf16),
            pltpu.VMEM((UPDATES, slots, per * ob, samples), bf16),
            pltpu.VMEM((samples // 128, K * ob, 128), f32),
            pltpu.VMEM((samples // 128, K * ob, 128), f32),
            pltpu.VMEM((K, 128), f32),
            pltpu.VMEM((UPDATES, slots * CORES, K * 2 * K // 128, 128), f32),
            dma((Z,)), dma((Z,)),
            dma((2 * M,)), dma((2 * M,)),
            dma((UPDATES,)), dma((UPDATES,)),
            dma((UPDATES,)), dma((UPDATES,)),
            dma((UPDATES,)), dma((UPDATES,)),
        ],
        compiler_params=pltpu.CompilerParams(
            collective_id=0, has_side_effects=True, vmem_limit_bytes=56 * 1024 * 1024
        ),
        name="inversion",
    )(inputs.T, observed, noise.reshape(UPDATES, K * ob, samples), w_in, b_in, w_out, b_out)
    return pl.pallas_call(
        place,
        out_shape=tuple(jax.ShapeDtypeStruct(own.shape, f32) for own in results),
        in_specs=[hbm] * 4,
        out_specs=(hbm,) * 4,
        scratch_shapes=[pltpu.VMEM(own.shape, f32) for own in results] + [dma((8,))],
        compiler_params=pltpu.CompilerParams(vmem_limit_bytes=56 * 1024 * 1024),
        name="place",
    )(*results)


def solution(mesh):
    placed = (
        P("dp", None),
        P("member", "dp"),
        P(None, None, "member", "dp"),
        P("member", None, "dp"),
        P("member", "dp"),
        P("member", None, "dp"),
        P("member", None),
    )
    return jax.shard_map(
        functools.partial(on_device, mesh.shape["member"], mesh.shape["dp"] // CORES),
        mesh=mesh,
        in_specs=placed,
        out_specs=(
            P("member", None, "dp"),
            P("member", "dp"),
            P("member", None, "dp"),
            P("member", None),
        ),
        check_vma=False,
    )
```
